256 devices in a mesh: win: 16 (over z, x_lo), space: 16 (over x_hi, y, core).
Axes of the slice: x: 4 (x_hi: 2, x_lo: 2; x = x_hi * 2 + x_lo), y: 4, z: 8, core: 2. Of those that a mesh axis runs over, the one named last changes fastest.
Arguments:
- first_guess: float32 [16, 2, 384, 384], P('win', None, 'space'), may hold values from -6 to 6
- forcing: float32 [384, 512], P('space'), may hold values from -6 to 6
- swirl: float32 [384], P('space'), may hold values from 0.1 to 1
- radial_op: float32 [384, 384], replicated, may hold values from -0.3125 to 0.3125
- obs_index: int32 [16, 8, 4096], P('win', None, 'space'), may hold values from 0 to 24575
- obs_value: float32 [16, 8, 4096], P('win', None, 'space'), may hold values from -6 to 6
- start_step: int32 [16], P('win'), may hold values from 0 to 63
Outputs:
- final_state: float32 [16, 2, 384, 384], P('win', None, 'space')
- misfit: float32 [16], P('win')
- forcing_gradient: float32 [384, 512], P('space')
The draws below stay inside these ranges and needn't reach their ends.
Inputs may be any that keep to these rules, and one draw needn't show every extreme that they name: `obs_index`: values of entries in block b of the last dimension name cells of the field rows held in radial block b, as the steps state.
All inputs are finite; a program needn't handle non-finite values.
Results may differ from the reference program's by a relative error of at most 0.0003.
Values sent between devices are 32-bit elements; how exact they have to be, the bound alone decides.
No kernel may reach another device: no remote copies, remote signals or barrier semaphores. Data moves between devices by JAX's collectives and lax.ppermute only.
A program may use at most 128 MiB of HBM per device.

```python
import math
import jax
import jax.numpy as jnp
from jax import lax

NR = 384
NT = 512
MODES = 192
AX = 2
STEPS = 8
ROT = 8
OBS_DEV = 256
KEEP = 384
WINDOWS = 16
NOBS = 4096
N_SPACE = 16


def place_ends(array, own_key, low, largest):
    longest = array.shape.index(max(array.shape))
    spots = []
    for shift in (0, 1):
        where = [jax.random.randint(jax.random.fold_in(own_key, axis), (), 0, length) for axis, length in enumerate(array.shape)]
        where[longest] = (where[longest] + shift) % array.shape[longest]
        spots.append(tuple(where))
    return array.at[spots[0]].set(low).at[spots[1]].set(largest)


def level_of(rng, extent, split, low, high):
    gain, own = 1.0, jax.random.fold_in(rng, 6)
    for axis_at, blocks in split:
        heights = jnp.exp(jax.random.uniform(jax.random.fold_in(own, axis_at), (blocks,), jnp.float32, low / len(split), high / len(split)))
        gain = gain * jnp.repeat(heights, extent[axis_at] // blocks).reshape([-1 if axis == axis_at else 1 for axis in range(len(extent))])
    return gain


def scatter_about(key, shape, width, reach, split=(), kind=jnp.bfloat16):
    array = width * jax.random.normal(key, shape, jnp.float32)
    if split:
        array = array * level_of(key, shape, split, -0.22, 0.18)
    return jnp.clip(array, -reach, reach).astype(kind)


def setup_inputs(seed: int = 0) -> dict:
    seeds = jax.random.split(jax.random.key(seed), 8)
    return {
        "first_guess": scatter_about(seeds[0], (WINDOWS, AX, NR, KEEP), 1.0, 6.0, ((0, 16), (2, 16)), jnp.float32),
        "forcing": scatter_about(seeds[1], (NR, NT), 1.0, 6.0, ((0, 16),), jnp.float32),
        "swirl": jnp.clip(jnp.exp(math.log(1.0) - 2.3025851 * jax.random.uniform(seeds[2], (NR,), jnp.float32) ** level_of(seeds[2], (NR,), ((0, 16),), -0.2, 0.2)), 0.1, 1.0),
        "radial_op": scatter_about(seeds[3], (NR, NR), NR ** -0.5, 0.3125, (), jnp.float32),
        "obs_index": place_ends(jax.random.randint(seeds[4], (WINDOWS, STEPS, NOBS), 0, AX * (NR // N_SPACE) * NT), jax.random.fold_in(seeds[4], 1), 0, (AX * (NR // N_SPACE) * NT) - 1).astype(jnp.int32),
        "obs_value": scatter_about(seeds[5], (WINDOWS, STEPS, NOBS), 1.0, 6.0, ((0, 16), (2, 16)), jnp.float32),
        "start_step": place_ends(jax.random.randint(seeds[6], (WINDOWS,), 0, NT // ROT), jax.random.fold_in(seeds[6], 1), 0, (NT // ROT) - 1).astype(jnp.int32),
    }


step_size = 0.25
radial_scale = 0.4
radial_damping = 0.4
axial_speed = 0.4
advection_gain = 0.2

def mode_numbers():
    slot_ids = jnp.arange(2 * MODES, dtype=jnp.int32)
    return jnp.where(slot_ids < MODES, slot_ids, slot_ids - MODES + 1)

def profile_weights(planes):
    centre = jnp.arange(planes, dtype=jnp.float32) + 0.5 - planes / 2.0
    return jnp.exp(-(centre * (4.0 / planes)) ** 2)

def synthesize(coeffs, derive):
    half_count = NT // 2 + 1
    zero_norm = 1.0 / math.sqrt(NT)
    mode_norm = math.sqrt(2.0 / NT)
    leading = coeffs.shape[:-1]
    cosines = coeffs[..., :MODES]
    sines = coeffs[..., MODES:]
    real_part = jnp.concatenate([NT * zero_norm * cosines[..., :1], 0.5 * NT * mode_norm * cosines[..., 1:], jnp.zeros(leading + (half_count - MODES,), coeffs.dtype)], -1)
    imag_part = jnp.concatenate([jnp.zeros(leading + (1,), coeffs.dtype), -0.5 * NT * mode_norm * sines, jnp.zeros(leading + (half_count - MODES - 1,), coeffs.dtype)], -1)
    if derive:
        wavenumber = 2.0 * math.pi / NT * jnp.arange(half_count, dtype=jnp.float32)
        real_part, imag_part = (-wavenumber * imag_part, wavenumber * real_part)
    return jnp.fft.irfft(lax.complex(real_part, imag_part), n=NT, axis=-1)

def analyze(source_field):
    spectrum = jnp.fft.rfft(source_field, axis=-1)
    zero_norm = 1.0 / math.sqrt(NT)
    mode_norm = math.sqrt(2.0 / NT)
    real_part = jnp.real(spectrum)
    imag_part = jnp.imag(spectrum)
    return jnp.concatenate([zero_norm * real_part[..., :1], mode_norm * real_part[..., 1:MODES], -mode_norm * imag_part[..., 1:MODES + 1]], -1)

def locate(sample_rows):
    radial_rows = NR // N_SPACE
    block_ids = jnp.arange(sample_rows.shape[-1], dtype=jnp.int32) // OBS_DEV
    plane_ids = sample_rows // (radial_rows * NT)
    radius_ids = block_ids * radial_rows + sample_rows // NT % radial_rows
    return (plane_ids * NR + radius_ids) * NT + sample_rows % NT

def run_window(forcing_field, phase_start, guess, flat_rows, values, swirl, radial_op):
    viscosity = (mode_numbers().astype(jnp.float32) / MODES) ** 2
    profile = profile_weights(AX)
    state = guess
    squares = jnp.zeros((), jnp.float32)
    for instant in range(STEPS):
        turn_cells = ROT * (phase_start + instant) % NT
        velocity = synthesize(state, False)
        derivative = synthesize(state, True)
        body_force = jnp.roll(forcing_field, turn_cells, axis=1)
        tendency = -(swirl[None, :, None] + advection_gain * velocity) * derivative + profile[:, None, None] * body_force[None]
        coupled = jnp.einsum('rs,ask->ark', radial_op, state, precision=lax.Precision.HIGHEST)
        upstream = jnp.concatenate([jnp.zeros_like(state[:1]), state[:-1]], 0)
        state = state + step_size * (analyze(tendency) + radial_scale * coupled - (radial_damping + axial_speed + viscosity) * state + axial_speed * upstream)
        sampled = synthesize(state, False).reshape(-1)[flat_rows[instant]]
        residual = sampled - values[instant]
        squares = squares + jnp.sum(residual * residual)
    return (state, 0.5 * squares)

def reference(first_guess, forcing, swirl, radial_op, obs_index, obs_value, start_step):

    def one_window(window_items):
        guess, sample_rows, values, phase_start = window_items
        flat_rows = locate(sample_rows)

        def window_cost(forcing_field):
            return run_window(forcing_field, phase_start, guess, flat_rows, values, swirl, radial_op)
        (final_field, squares), pull = jax.vjp(window_cost, forcing)
        pulled_back = pull((jnp.zeros_like(final_field), jnp.ones_like(squares)))[0]
        return (final_field, squares / (STEPS * NOBS), pulled_back)
    finals, misfits, pulled_all = lax.map(one_window, (first_guess, obs_index, obs_value, start_step))
    return (finals, misfits, lax.optimization_barrier(jnp.sum(pulled_all, 0)))
```

```python
import math

import jax
import jax.numpy as jnp
import ml_dtypes
import numpy as np
from jax import lax
from jax.experimental import pallas as pl
from jax.experimental.pallas import tpu as pltpu
from jax.sharding import PartitionSpec as P

MODES = 192
STEPS = 8
ROT = 8
NT = 512
NR = 384
AX = 2
HALF = NT // 2
BLOCKS = 16
QR = NR // BLOCKS
OBS = 256
ROWS = AX * NR
COEF = 2 * HALF
VMEM_LIMIT = 60 * 1024 * 1024

step_size = 0.25
radial_scale = 0.4
radial_damping = 0.4
axial_speed = 0.4
advection_gain = 0.2
PROFILE = [math.exp(-(((a + 0.5 - AX / 2.0) * (4.0 / AX)) ** 2)) for a in range(AX)]

OMEGA = 2.0 * math.pi / NT
PHI = OMEGA * np.arange(HALF) / 2.0


def split_np(table):
    high = table.astype(ml_dtypes.bfloat16)
    low = (table - high.astype(np.float64)).astype(ml_dtypes.bfloat16)
    return high, low


def half_tables():
    m = np.arange(HALF)[:, None].astype(np.float64)
    theta = np.arange(HALF)[None, :] + 0.5
    norm = np.where(m == 0, 1.0 / math.sqrt(NT), math.sqrt(2.0 / NT))
    cosine = norm * np.cos(OMEGA * m * theta)
    sine = norm * np.sin(OMEGA * m * theta)
    slope = OMEGA * m
    kept = m < MODES
    last = m == MODES
    sin_phi, cos_phi = math.sin(PHI[MODES]), math.cos(PHI[MODES])
    even_u = np.where(kept, cosine, np.where(last, -sin_phi * cosine, 0.0))
    odd_u = np.where(kept & (m > 0), sine, np.where(last, cos_phi * sine, 0.0))
    odd_v = np.where(kept, -slope * sine, np.where(last, sin_phi * slope * sine, 0.0))
    even_v = np.where(kept & (m > 0), slope * cosine, np.where(last, cos_phi * slope * cosine, 0.0))
    from_cos = np.concatenate([even_u, odd_v], 1)
    from_sin = np.concatenate([odd_u, even_v], 1)
    return from_cos, from_sin


def whole_table():
    m = np.arange(HALF)[:, None].astype(np.float64)
    theta = np.arange(NT)[None, :] + 0.5
    norm = np.where(m == 0, 1.0 / math.sqrt(NT), math.sqrt(2.0 / NT))
    cosine = np.where(m <= MODES, norm * np.cos(OMEGA * m * theta), 0.0)
    sine = np.where((m <= MODES) & (m > 0), norm * np.sin(OMEGA * m * theta), 0.0)
    return np.concatenate([cosine, sine], 0)


def lane_rows():
    m = np.arange(HALF)
    kept = (m >= 1) & (m < MODES)
    last = m == MODES
    cos_phi, sin_phi = np.cos(PHI), np.sin(PHI)
    rows = np.zeros((16, HALF))
    rows[0] = np.where(kept, cos_phi, np.where(m == 0, 1.0, 0.0))
    rows[1] = np.where(kept, -sin_phi, np.where(last, 1.0, 0.0))
    rows[2] = np.where(kept, sin_phi, 0.0)
    rows[3] = np.where(kept, cos_phi, np.where(last, 1.0, 0.0))
    rows[4] = np.where(kept, cos_phi, np.where(m == 0, 1.0, 0.0))
    rows[5] = np.where(kept, sin_phi, 0.0)
    rows[6] = np.where(kept, -sin_phi, 0.0)
    rows[7] = np.where(kept, cos_phi, np.where(last, 1.0, 0.0))
    rows[8] = np.where(m <= MODES, 1.0 - step_size * (radial_damping + axial_speed + (m / MODES) ** 2), 0.0)
    rows[9] = np.where(last, 1.0, 0.0)
    return rows.astype(np.float32)


def turn_tables(phase_start):
    m = jnp.arange(HALF, dtype=jnp.int32)[None, :]
    cells = ROT * (phase_start + jnp.arange(STEPS, dtype=jnp.int32))[:, None]
    angles = OMEGA * ((m * cells) % NT).astype(jnp.float32)
    cosine, sine = jnp.cos(angles), jnp.sin(angles)
    sin_phi, cos_phi = math.sin(PHI[MODES]), math.cos(PHI[MODES])
    last = m == MODES
    first = -sin_phi * cosine + cos_phi * sine
    second = sin_phi * sine + cos_phi * cosine
    forward = [
        jnp.where(last, first, cosine),
        jnp.where(last, second, -sine),
        jnp.where(last, first, sine),
        jnp.where(last, second, cosine),
    ]
    back = [
        forward[0],
        jnp.where(last, 0.0, sine),
        forward[1],
        jnp.where(last, 0.0, cosine),
    ]
    keep = (m <= MODES).astype(jnp.float32)
    return jnp.stack([row * keep for row in forward + back], 1)


def split(x):
    high = x.astype(jnp.bfloat16)
    return high, (x - high.astype(jnp.float32)).astype(jnp.bfloat16)


def mm(a, b):
    return jnp.dot(a, b, preferred_element_type=jnp.float32)


def mm3(xh, xl, th, tl):
    return mm(xh, th) + mm(xl, th) + mm(xh, tl)


def kernel(
    place, turns, lanes, radial_op, tch, tcl, tsh, tsl, bch, bcl, bsh, bsl, fth, ftl, gth, gtl,
    p0, p1, p2, p3, p4, q0, q1, q2, q3, q4,
    final_out, grad_out, miss_out,
    state, high, rad, hist_u, hist_v, inject, rl, rtl, swirl, forced, obs_i, obs_v, gsum, msum,
):
    me = place[0]
    core = me % 2
    across = me // 8
    up = (me // 2) % 4

    def block_of(d, flip_x, flip_core):
        y = (up + 4 - d) % 4
        x = 1 - across if flip_x else across
        c = 1 - core if flip_core else core
        return x * 8 + y * 2 + c

    sources = [(p0, 0, 0, False, False), (p1, 0, 0, True, False), (q0, 0, 0, False, True), (q1, 0, 0, True, True)]
    for d, (pd, qd) in enumerate(((p2, q2), (p3, q3), (p4, q4)), 1):
        sources += [(pd, 0, d, False, False), (pd, QR, d, True, False), (qd, 0, d, False, True), (qd, QR, d, True, True)]

    def lane(i):
        return lanes[i:i + 1, :]

    square = lax.broadcasted_iota(jnp.int32, (QR, 128), 0) == lax.broadcasted_iota(jnp.int32, (QR, 128), 1)
    for ref, row, d, flip_x, flip_core in sources:
        block = block_of(d, flip_x, flip_core)
        at = pl.multiple_of(block * QR, 8)
        for a in range(AX):
            first = ref[row:row + QR, 384 * a:384 * a + HALF]
            second = pltpu.roll(ref[row:row + QR, 384 * a + 128:384 * a + 384], 193, 1)
            spot = pl.multiple_of(a * NR + at, 8)
            state[pl.ds(spot, QR), 0:HALF] = first * lane(0) + second * lane(1)
            state[pl.ds(spot, QR), HALF:COEF] = first * lane(2) + second * lane(3)
        forced[pl.ds(at, QR), :] = ref[row:row + QR, 768:1280]
        spread = jnp.where(square, ref[row + 16:row + 17, 1280:1408], 0.0)
        swirl[pl.ds(at, QR), :] = jnp.broadcast_to(jnp.sum(spread, 1, keepdims=True), (QR, 128))
        if not flip_core:
            slot = pl.multiple_of((block // 2) * STEPS, 8)
            obs_i[pl.ds(slot, STEPS), :] = ref[row:row + 8, 1280:1536].astype(jnp.int32)
            obs_v[pl.ds(slot, STEPS), :] = ref[row + 8:row + 16, 1280:1536]

    fh, fl = split(forced[...])
    forced[...] = mm3(fh, fl, fth[...], ftl[...]) * step_size

    scaled = (step_size * radial_scale) * radial_op[...]
    rh, rlow = split(scaled)
    rl[:, 0:NR], rl[:, NR:2 * NR], rl[:, 2 * NR:] = rh, rlow, rh
    th, tlow = split(scaled.T)
    rtl[:, 0:NR], rtl[:, NR:2 * NR], rtl[:, 2 * NR:] = th, tlow, th
    inject[...] = jnp.zeros_like(inject)
    gsum[...] = jnp.zeros_like(gsum)
    msum[...] = jnp.zeros_like(msum)

    mark = lane(9)
    decay = lane(8)
    reach = step_size * axial_speed

    def store_split(a):
        h, l = split(state[a * NR:(a + 1) * NR, :])
        high[a, 0:NR, :] = h
        high[a, NR:2 * NR, :] = h
        high[a, 2 * NR:, :] = l

    def couple(operator):
        for a in range(AX):
            rad[a] = mm(operator[...], high[a])

    def halves(a, part):
        lanes_of = slice(0, HALF) if part == 0 else slice(HALF, COEF)
        return high[a, 0:NR, lanes_of], high[a, 2 * NR:, lanes_of]

    def fold(pc, ps):
        return pc + mark * ps, ps + mark * pc

    def expand_u(a):
        ch, cl = halves(a, 0)
        sh, sl = halves(a, 1)
        eu = mm3(ch, cl, tch[:, 0:HALF], tcl[:, 0:HALF])
        ou = mm3(sh, sl, tsh[:, 0:HALF], tsl[:, 0:HALF])
        return eu, ou

    def forward_step(k):
        couple(rl)
        body_c = turns[k, 0:1, :] * forced[:, 0:HALF] + turns[k, 1:2, :] * forced[:, HALF:COEF]
        body_s = turns[k, 2:3, :] * forced[:, 0:HALF] + turns[k, 3:4, :] * forced[:, HALF:COEF]
        sw = jnp.concatenate([swirl[...], swirl[...]], 1)
        for a in range(AX - 1, -1, -1):
            rows = slice(a * NR, (a + 1) * NR)
            ch, cl = halves(a, 0)
            sh, sl = halves(a, 1)
            from_cos = mm3(ch, cl, tch[...], tcl[...])
            from_sin = mm3(sh, sl, tsh[...], tsl[...])
            eu, ov = from_cos[:, 0:HALF], from_cos[:, HALF:]
            ou, ev = from_sin[:, 0:HALF], from_sin[:, HALF:]
            hist_u[k, rows, 0:HALF] = eu
            hist_u[k, rows, HALF:] = ou
            hist_v[k, rows, 0:HALF] = ev
            hist_v[k, rows, HALF:] = ov
            speed_e = sw + advection_gain * eu
            speed_o = advection_gain * ou
            ge = -(speed_e * ev + speed_o * ov)
            go = -(speed_e * ov + speed_o * ev)
            geh, gel = split(ge)
            goh, gol = split(go)
            pc, ps = fold(mm3(geh, gel, bch[0:HALF, :], bcl[0:HALF, :]), mm3(goh, gol, bsh[0:HALF, :], bsl[0:HALF, :]))
            new_c = decay * state[rows, 0:HALF] + pc + PROFILE[a] * body_c + rad[a, :, 0:HALF]
            new_s = decay * state[rows, HALF:] + ps + PROFILE[a] * body_s + rad[a, :, HALF:]
            if a > 0:
                before = slice((a - 1) * NR, a * NR)
                new_c = new_c + reach * state[before, 0:HALF]
                new_s = new_s + reach * state[before, HALF:]
            state[rows, 0:HALF] = new_c
            state[rows, HALF:] = new_s
            store_split(a)

    tall = lax.broadcasted_iota(jnp.int32, (NT, OBS), 0)
    short = lax.broadcasted_iota(jnp.int32, (AX * QR, OBS), 0)

    def sample(k):
        held = k % STEPS

        def one(b, total):
            block = 2 * b + core
            cell = obs_i[pl.ds(b * STEPS + k - 1, 1), :]
            value = obs_v[pl.ds(b * STEPS + k - 1, 1), :]
            column = cell & (NT - 1)
            column = jnp.where(column < HALF, column, NT + HALF - 1 - column)
            which = (tall == column).astype(jnp.float32).astype(jnp.bfloat16)
            at_row = short == (cell >> 9)
            parts = []
            for a in range(AX):
                spot = pl.multiple_of(a * NR + block * QR, 8)
                eu = hist_u[held, pl.ds(spot, QR), 0:HALF]
                ou = hist_u[held, pl.ds(spot, QR), HALF:]
                parts.append(jnp.concatenate([eu + ou, eu - ou], 1))
            uh, ul = split(jnp.concatenate(parts, 0))
            picked = mm(uh, which) + mm(ul, which)
            miss = jnp.sum(jnp.where(at_row, picked, 0.0), 0, keepdims=True) - value
            eh, el = split(jnp.where(at_row, miss, 0.0))
            dims = (((1,), (1,)), ((), ()))
            back = lax.dot_general(eh, which, dims, preferred_element_type=jnp.float32)
            back = back + lax.dot_general(el, which, dims, preferred_element_type=jnp.float32)
            plus, minus = back[:, 0:HALF], back[:, HALF:]
            grow = 0.5 / step_size
            for a in range(AX):
                spot = pl.multiple_of(a * NR + block * QR, 8)
                own = slice(a * QR, (a + 1) * QR)
                inject[k - 1, pl.ds(spot, QR), 0:HALF] = grow * (plus[own] + minus[own])
                inject[k - 1, pl.ds(spot, QR), HALF:] = grow * (plus[own] - minus[own])
            return total + miss * miss

        msum[...] += lax.fori_loop(0, BLOCKS // 2, one, jnp.zeros((1, OBS), jnp.float32), unroll=4)

    for a in range(AX):
        store_split(a)
    forward_step(0)

    def onward(k, carry):
        forward_step(k)
        sample(k)
        return carry

    lax.fori_loop(1, STEPS, onward, 0)
    for a in range(AX):
        rows = slice(a * NR, (a + 1) * NR)
        eu, ou = expand_u(a)
        hist_u[0, rows, 0:HALF] = eu
        hist_u[0, rows, HALF:] = ou
    sample(STEPS)
    miss_out[...] = jnp.broadcast_to(jnp.sum(msum[...], 1, keepdims=True), miss_out.shape)

    mine = pl.multiple_of(me * QR, 8)
    for a in range(AX):
        spot = pl.multiple_of(a * NR + mine, 8)
        cos_part = state[pl.ds(spot, QR), 0:HALF]
        sin_part = state[pl.ds(spot, QR), HALF:]
        plain_c = cos_part * lane(4) + sin_part * lane(5)
        plain_s = pltpu.roll(cos_part * lane(6) + sin_part * lane(7), 63, 1)
        at_lane = lax.broadcasted_iota(jnp.int32, (QR, 128), 1)
        final_out[a, :, 0:128] = plain_c[:, 0:128]
        final_out[a, :, 128:256] = jnp.where(at_lane < 64, plain_c[:, 128:], plain_s[:, 0:128])
        final_out[a, :, 256:384] = plain_s[:, 128:]

    chip = pl.multiple_of((me - core) * QR, 8)

    def gather_gradient(k):
        wc = jnp.zeros((2 * QR, HALF), jnp.float32)
        ws = wc
        for a in range(AX):
            spot = pl.multiple_of(a * NR + chip, 8)
            wc = wc + (step_size * PROFILE[a]) * state[pl.ds(spot, 2 * QR), 0:HALF]
            ws = ws + (step_size * PROFILE[a]) * state[pl.ds(spot, 2 * QR), HALF:]
        gsum[:, 0:HALF] += turns[k, 4:5, :] * wc + turns[k, 5:6, :] * ws
        gsum[:, HALF:] += turns[k, 6:7, :] * wc + turns[k, 7:8, :] * ws

    for a in range(AX):
        rows = slice(a * NR, (a + 1) * NR)
        eh, el = split(inject[STEPS - 1, rows, 0:HALF])
        oh, ol = split(inject[STEPS - 1, rows, HALF:])
        lc, ls = fold(mm3(eh, el, bch[0:HALF, :], bcl[0:HALF, :]), mm3(oh, ol, bsh[0:HALF, :], bsl[0:HALF, :]))
        state[rows, 0:HALF] = lc
        state[rows, HALF:] = ls
        store_split(a)

    def backward_step(k):
        couple(rtl)
        sw = jnp.concatenate([swirl[...], swirl[...]], 1)
        for a in range(AX):
            rows = slice(a * NR, (a + 1) * NR)
            eq, oq = expand_u(a)
            eu, ou = hist_u[k, rows, 0:HALF], hist_u[k, rows, HALF:]
            ev, ov = hist_v[k, rows, 0:HALF], hist_v[k, rows, HALF:]
            speed_e = sw + advection_gain * eu
            speed_o = advection_gain * ou
            tve = -(speed_e * eq + speed_o * oq)
            tvo = -(speed_e * oq + speed_o * eq)
            eq = advection_gain * eq
            oq = advection_gain * oq
            tue = inject[k - 1, rows, 0:HALF] - (ev * eq + ov * oq)
            tuo = inject[k - 1, rows, HALF:] - (ev * oq + ov * eq)
            ueh, uel = split(tue)
            uoh, uol = split(tuo)
            veh, vel = split(tve)
            voh, vol = split(tvo)
            pc = mm3(ueh, uel, bch[0:HALF, :], bcl[0:HALF, :]) + mm3(voh, vol, bch[HALF:, :], bcl[HALF:, :])
            ps = mm3(uoh, uol, bsh[0:HALF, :], bsl[0:HALF, :]) + mm3(veh, vel, bsh[HALF:, :], bsl[HALF:, :])
            pc, ps = fold(pc, ps)
            new_c = decay * state[rows, 0:HALF] + pc + rad[a, :, 0:HALF]
            new_s = decay * state[rows, HALF:] + ps + rad[a, :, HALF:]
            if a < AX - 1:
                after = slice((a + 1) * NR, (a + 2) * NR)
                new_c = new_c + reach * state[after, 0:HALF]
                new_s = new_s + reach * state[after, HALF:]
            state[rows, 0:HALF] = new_c
            state[rows, HALF:] = new_s
            store_split(a)

    def inward(i, carry):
        k = STEPS - 1 - i
        gather_gradient(k)
        backward_step(k)
        return carry

    lax.fori_loop(0, STEPS - 1, inward, 0)
    gather_gradient(0)
    gh, gl = split(gsum[...])
    grad_out[...] = mm3(gh, gl, gth[...], gtl[...])


def window_step(place, turns, radial_op, pieces):
    from_cos, from_sin = half_tables()
    whole = whole_table()
    tables = []
    for table in (from_cos, from_sin, 2.0 * step_size * from_cos.T, 2.0 * step_size * from_sin.T, whole.T, whole):
        tables += [jnp.asarray(part) for part in split_np(table)]
    operands = [place, turns, jnp.asarray(lane_rows()), radial_op, *tables, *pieces]
    vmem = pl.BlockSpec(memory_space=pltpu.VMEM)
    f32, bf16 = jnp.float32, jnp.bfloat16
    return pl.pallas_call(
        kernel,
        out_shape=(
            jax.ShapeDtypeStruct((AX, QR, 384), f32),
            jax.ShapeDtypeStruct((2 * QR, NT), f32),
            jax.ShapeDtypeStruct((8, 128), f32),
        ),
        in_specs=[pl.BlockSpec(memory_space=pltpu.SMEM)] + [vmem] * (len(operands) - 1),
        out_specs=(vmem, vmem, vmem),
        scratch_shapes=[
            pltpu.VMEM((ROWS, COEF), f32),
            pltpu.VMEM((AX, 3 * NR, COEF), bf16),
            pltpu.VMEM((AX, NR, COEF), f32),
            pltpu.VMEM((STEPS, ROWS, COEF), f32),
            pltpu.VMEM((STEPS, ROWS, COEF), f32),
            pltpu.VMEM((STEPS, ROWS, COEF), f32),
            pltpu.VMEM((NR, 3 * NR), bf16),
            pltpu.VMEM((NR, 3 * NR), bf16),
            pltpu.VMEM((NR, 128), f32),
            pltpu.VMEM((NR, COEF), f32),
            pltpu.VMEM((BLOCKS // 2 * STEPS, OBS), jnp.int32),
            pltpu.VMEM((BLOCKS // 2 * STEPS, OBS), f32),
            pltpu.VMEM((2 * QR, COEF), f32),
            pltpu.VMEM((1, OBS), f32),
        ],
        compiler_params=pltpu.CompilerParams(vmem_limit_bytes=VMEM_LIMIT),
    )(*operands)


def per_device(first_guess, forcing, swirl, radial_op, obs_index, obs_value, start_step):
    me = lax.axis_index("space")

    def space_swap(x, bits):
        return lax.ppermute(x, "space", [(i, i ^ bits) for i in range(BLOCKS)])

    def space_turn(x, d):
        return lax.ppermute(x, "space", [(i, i // 8 * 8 + (i + 2 * d) % 8) for i in range(BLOCKS)])

    def win_send(x, where):
        return lax.ppermute(x, "win", [(i, where(i)) for i in range(16)])

    extra = jnp.concatenate(
        [
            obs_index[0].astype(jnp.float32),
            obs_value[0],
            jnp.pad(swirl[None, :], ((0, 7), (0, OBS - QR))),
        ],
        0,
    )
    message = jnp.concatenate([first_guess[0, 0], first_guess[0, 1], forcing, extra], 1)
    other_x = space_swap(message, 8)
    both = jnp.concatenate([message, other_x], 0)
    pieces = [message, other_x] + [space_turn(both, d) for d in (1, 2, 3)]
    pieces += [space_swap(piece, 1) for piece in pieces]

    turns = turn_tables(start_step[0])
    final, grad, misses = window_step(me.astype(jnp.int32).reshape(1), turns, radial_op, pieces)

    core = me % 2
    for_other = lax.dynamic_slice_in_dim(grad, (1 - core) * QR, QR, 0)
    own = lax.dynamic_slice_in_dim(grad, core * QR, QR, 0)
    misfit = (misses + space_swap(misses, 1))[0, 0:1] * (0.5 / (STEPS * BLOCKS * OBS))
    total = own + space_swap(for_other, 1)
    near = [win_send(total, lambda i, f=f: i ^ f) for f in (1, 2, 3)]
    total = total + near[0] + near[1] + near[2]
    far = [win_send(total, lambda i, d=d: (i + 2 * d) % 16) for d in (2, 4, 6)]
    total = total + far[0] + far[1] + far[2]
    return final[None], misfit, total


def solution(mesh):
    return jax.shard_map(
        per_device,
        mesh=mesh,
        in_specs=(
            P("win", None, "space", None),
            P("space", None),
            P("space"),
            P(),
            P("win", None, "space"),
            P("win", None, "space"),
            P("win"),
        ),
        out_specs=(P("win", None, "space", None), P("win"), P("space", None)),
        check_vma=False,
    )
```

```python
import math

import jax
import jax.numpy as jnp
import ml_dtypes
import numpy as np
from jax import lax
from jax.experimental import pallas as pl
from jax.experimental.pallas import tpu as pltpu
from jax.sharding import PartitionSpec as P

MODES = 192
STEPS = 8
ROT = 8
NT = 512
NR = 384
AX = 2
HALF = NT // 2
BLOCKS = 16
QR = NR // BLOCKS
OBS = 256
ROWS = AX * NR
COEF = 2 * HALF
GROUP = 8
CHUNK = 384
VMEM_LIMIT = 60 * 1024 * 1024

step_size = 0.25
radial_scale = 0.4
radial_damping = 0.4
axial_speed = 0.4
advection_gain = 0.2
PROFILE = [math.exp(-(((a + 0.5 - AX / 2.0) * (4.0 / AX)) ** 2)) for a in range(AX)]

OMEGA = 2.0 * math.pi / NT
PHI = OMEGA * np.arange(HALF) / 2.0


def split_np(table):
    high = table.astype(ml_dtypes.bfloat16)
    low = (table - high.astype(np.float64)).astype(ml_dtypes.bfloat16)
    return high, low


def half_tables():
    m = np.arange(HALF)[:, None].astype(np.float64)
    theta = np.arange(HALF)[None, :] + 0.5
    norm = np.where(m == 0, 1.0 / math.sqrt(NT), math.sqrt(2.0 / NT))
    cosine = norm * np.cos(OMEGA * m * theta)
    sine = norm * np.sin(OMEGA * m * theta)
    slope = OMEGA * m
    kept = m < MODES
    last = m == MODES
    sin_phi, cos_phi = math.sin(PHI[MODES]), math.cos(PHI[MODES])
    even_u = np.where(kept, cosine, np.where(last, -sin_phi * cosine, 0.0))
    odd_u = np.where(kept & (m > 0), sine, np.where(last, cos_phi * sine, 0.0))
    odd_v = np.where(kept, -slope * sine, np.where(last, sin_phi * slope * sine, 0.0))
    even_v = np.where(kept & (m > 0), slope * cosine, np.where(last, cos_phi * slope * cosine, 0.0))
    from_cos = np.concatenate([even_u, odd_v], 1)
    from_sin = np.concatenate([odd_u, even_v], 1)
    return from_cos, from_sin


def whole_table():
    m = np.arange(HALF)[:, None].astype(np.float64)
    theta = np.arange(NT)[None, :] + 0.5
    norm = np.where(m == 0, 1.0 / math.sqrt(NT), math.sqrt(2.0 / NT))
    cosine = np.where(m <= MODES, norm * np.cos(OMEGA * m * theta), 0.0)
    sine = np.where((m <= MODES) & (m > 0), norm * np.sin(OMEGA * m * theta), 0.0)
    return np.concatenate([cosine, sine], 0)


def lane_rows():
    m = np.arange(HALF)
    kept = (m >= 1) & (m < MODES)
    last = m == MODES
    cos_phi, sin_phi = np.cos(PHI), np.sin(PHI)
    rows = np.zeros((16, HALF))
    rows[0] = np.where(kept, cos_phi, np.where(m == 0, 1.0, 0.0))
    rows[1] = np.where(kept, -sin_phi, np.where(last, 1.0, 0.0))
    rows[2] = np.where(kept, sin_phi, 0.0)
    rows[3] = np.where(kept, cos_phi, np.where(last, 1.0, 0.0))
    rows[4] = np.where(kept, cos_phi, np.where(m == 0, 1.0, 0.0))
    rows[5] = np.where(kept, sin_phi, 0.0)
    rows[6] = np.where(kept, -sin_phi, 0.0)
    rows[7] = np.where(kept, cos_phi, np.where(last, 1.0, 0.0))
    rows[8] = np.where(m <= MODES, 1.0 - step_size * (radial_damping + axial_speed + (m / MODES) ** 2), 0.0)
    rows[9] = np.where(last, 1.0, 0.0)
    return rows.astype(np.float32)


def turn_tables(phase_start):
    m = jnp.arange(HALF, dtype=jnp.int32)[None, :]
    cells = ROT * (phase_start + jnp.arange(STEPS, dtype=jnp.int32))[:, None]
    angles = OMEGA * ((m * cells) % NT).astype(jnp.float32)
    cosine, sine = jnp.cos(angles), jnp.sin(angles)
    sin_phi, cos_phi = math.sin(PHI[MODES]), math.cos(PHI[MODES])
    last = m == MODES
    first = -sin_phi * cosine + cos_phi * sine
    second = sin_phi * sine + cos_phi * cosine
    forward = [
        jnp.where(last, first, cosine),
        jnp.where(last, second, -sine),
        jnp.where(last, first, sine),
        jnp.where(last, second, cosine),
    ]
    back = [
        forward[0],
        jnp.where(last, 0.0, sine),
        forward[1],
        jnp.where(last, 0.0, cosine),
    ]
    keep = (m <= MODES).astype(jnp.float32)
    return jnp.stack([row * keep for row in forward + back], 1)


def split(x):
    high = x.astype(jnp.bfloat16)
    return high, (x - high.astype(jnp.float32)).astype(jnp.bfloat16)


def mm(a, b):
    return jnp.dot(a, b, preferred_element_type=jnp.float32)


def mm3(xh, xl, th, tl):
    return mm(xh, th) + mm(xl, th) + mm(xh, tl)


def kernel(
    place, turns, lanes, radial_op, tch, tcl, tsh, tsl, bch, bcl, bsh, bsl, fth, ftl, gth, gtl,
    p0, p1, p2, p3, p4, q0, q1, q2, q3, q4,
    final_out, keep_out, send_out,
    state, high, rad, hist_u, hist_v, inject, rl, rtl, swirl, forced, obs_i, obs_v, gsum, msum,
):
    me = place[0]
    core = me % 2
    across = me // 8
    up = (me // 2) % 4

    def block_of(d, flip_x, flip_core):
        y = (up + 4 - d) % 4
        x = 1 - across if flip_x else across
        c = 1 - core if flip_core else core
        return x * 8 + y * 2 + c

    sources = [(p0, 0, 0, False, False), (p1, 0, 0, True, False), (q0, 0, 0, False, True), (q1, 0, 0, True, True)]
    for d, (pd, qd) in enumerate(((p2, q2), (p3, q3), (p4, q4)), 1):
        sources += [(pd, 0, d, False, False), (pd, QR, d, True, False), (qd, 0, d, False, True), (qd, QR, d, True, True)]

    def lane(i):
        return lanes[i:i + 1, :]

    square = lax.broadcasted_iota(jnp.int32, (QR, 128), 0) == lax.broadcasted_iota(jnp.int32, (QR, 128), 1)
    for ref, row, d, flip_x, flip_core in sources:
        block = block_of(d, flip_x, flip_core)
        at = pl.multiple_of(block * QR, 8)
        for a in range(AX):
            first = ref[row:row + QR, 384 * a:384 * a + HALF]
            second = pltpu.roll(ref[row:row + QR, 384 * a + 128:384 * a + 384], 193, 1)
            spot = pl.multiple_of(a * NR + at, 8)
            state[pl.ds(spot, QR), 0:HALF] = first * lane(0) + second * lane(1)
            state[pl.ds(spot, QR), HALF:COEF] = first * lane(2) + second * lane(3)
        forced[pl.ds(at, QR), :] = ref[row:row + QR, 768:1280]
        spread = jnp.where(square, ref[row + 16:row + 17, 1280:1408], 0.0)
        swirl[pl.ds(at, QR), :] = jnp.broadcast_to(jnp.sum(spread, 1, keepdims=True), (QR, 128))
        if not flip_core:
            slot = pl.multiple_of((block // 2) * STEPS, 8)
            obs_i[pl.ds(slot, STEPS), :] = ref[row:row + 8, 1280:1536].astype(jnp.int32)
            obs_v[pl.ds(slot, STEPS), :] = ref[row + 8:row + 16, 1280:1536]

    fh, fl = split(forced[...])
    forced[...] = mm3(fh, fl, fth[...], ftl[...]) * step_size

    scaled = (step_size * radial_scale) * radial_op[...]
    rh, rlow = split(scaled)
    rl[:, 0:NR], rl[:, NR:2 * NR], rl[:, 2 * NR:] = rh, rlow, rh
    th, tlow = split(scaled.T)
    rtl[:, 0:NR], rtl[:, NR:2 * NR], rtl[:, 2 * NR:] = th, tlow, th
    gsum[...] = jnp.zeros_like(gsum)
    msum[...] = jnp.zeros_like(msum)

    mark = lane(9)
    decay = lane(8)
    reach = step_size * axial_speed

    def store_split(a, r):
        h, l = split(state[a * NR + r:a * NR + r + CHUNK, :])
        high[a, r:r + CHUNK, :] = h
        high[a, NR + r:NR + r + CHUNK, :] = h
        high[a, 2 * NR + r:2 * NR + r + CHUNK, :] = l

    def couple(operator):
        for a in range(AX):
            rad[a] = mm(operator[...], high[a])

    def halves(a, r, part):
        lanes_of = slice(0, HALF) if part == 0 else slice(HALF, COEF)
        return high[a, r:r + CHUNK, lanes_of], high[a, 2 * NR + r:2 * NR + r + CHUNK, lanes_of]

    def fold(pc, ps):
        return pc + mark * ps, ps + mark * pc

    def expand_u(a, r):
        ch, cl = halves(a, r, 0)
        sh, sl = halves(a, r, 1)
        eu = mm3(ch, cl, tch[:, 0:HALF], tcl[:, 0:HALF])
        ou = mm3(sh, sl, tsh[:, 0:HALF], tsl[:, 0:HALF])
        return eu, ou

    def forward_step(k):
        expanded = [None, None]
        fields = [None, None]
        for a in range(AX - 1, -1, -1):
            ch, cl = halves(a, 0, 0)
            sh, sl = halves(a, 0, 1)
            expanded[a] = (mm3(ch, cl, tch[...], tcl[...]), mm3(sh, sl, tsh[...], tsl[...]))
        sw = jnp.concatenate([swirl[...], swirl[...]], 1)
        for a in range(AX - 1, -1, -1):
            rows = slice(a * NR, (a + 1) * NR)
            from_cos, from_sin = expanded[a]
            eu, ov = from_cos[:, 0:HALF], from_cos[:, HALF:]
            ou, ev = from_sin[:, 0:HALF], from_sin[:, HALF:]
            hist_u[k, rows, 0:HALF] = eu
            hist_u[k, rows, HALF:] = ou
            hist_v[k, rows, 0:HALF] = ev
            hist_v[k, rows, HALF:] = ov
            speed_e = sw + advection_gain * eu
            speed_o = advection_gain * ou
            fields[a] = split(-(speed_e * ev + speed_o * ov)) + split(-(speed_e * ov + speed_o * ev))
            rad[a] = mm(rl[...], high[a])
        for a in range(AX - 1, -1, -1):
            rows = slice(a * NR, (a + 1) * NR)
            geh, gel, goh, gol = fields[a]
            pc, ps = fold(mm3(geh, gel, bch[0:HALF, :], bcl[0:HALF, :]), mm3(goh, gol, bsh[0:HALF, :], bsl[0:HALF, :]))
            force_c, force_s = forced[:, 0:HALF], forced[:, HALF:COEF]
            body_c = turns[k, 0:1, :] * force_c + turns[k, 1:2, :] * force_s
            body_s = turns[k, 2:3, :] * force_c + turns[k, 3:4, :] * force_s
            new_c = decay * state[rows, 0:HALF] + pc + PROFILE[a] * body_c + rad[a, :, 0:HALF]
            new_s = decay * state[rows, HALF:] + ps + PROFILE[a] * body_s + rad[a, :, HALF:]
            if a > 0:
                before = slice(rows.start - NR, rows.stop - NR)
                new_c = new_c + reach * state[before, 0:HALF]
                new_s = new_s + reach * state[before, HALF:]
            state[rows, 0:HALF] = new_c
            state[rows, HALF:] = new_s
            store_split(a, 0)

    tall = lax.broadcasted_iota(jnp.int32, (HALF, OBS), 0).astype(jnp.float32).astype(jnp.bfloat16)
    short = lax.broadcasted_iota(jnp.int32, (AX * QR, OBS), 0)
    one_wide = jnp.ones((HALF, OBS), jnp.bfloat16)
    zero_wide = jnp.zeros((HALF, OBS), jnp.bfloat16)

    def sample(k):
        held = k % STEPS

        dims = (((1,), (1,)), ((), ()))

        def group(first_block):
            blocks = range(first_block, first_block + GROUP)
            ats, values, whiches, picks = [], [], [], []
            for b in blocks:
                block = 2 * b + core
                cell = obs_i[pl.ds(b * STEPS + k - 1, 1), :]
                values.append(obs_v[pl.ds(b * STEPS + k - 1, 1), :])
                column = cell & (NT - 1)
                in_first = column < HALF
                first = jnp.where(in_first, column, -1).astype(jnp.float32).astype(jnp.bfloat16)
                second = jnp.where(in_first, -1, NT - 1 - column).astype(jnp.float32).astype(jnp.bfloat16)
                which = jnp.concatenate(
                    [jnp.where(tall == first, one_wide, zero_wide), jnp.where(tall == second, one_wide, zero_wide)], 0
                )
                whiches.append(which)
                ats.append(short == (cell >> 9))
                parts = []
                for a in range(AX):
                    spot = pl.multiple_of(a * NR + block * QR, 8)
                    eu = hist_u[held, pl.ds(spot, QR), 0:HALF]
                    ou = hist_u[held, pl.ds(spot, QR), HALF:]
                    parts.append(jnp.concatenate([eu + ou, eu - ou], 1))
                uh, ul = split(jnp.concatenate(parts, 0))
                picks.append(mm(jnp.concatenate([uh, ul], 0), which))
            errors, total = [], 0.0
            for at_row, value, picked in zip(ats, values, picks):
                picked = picked[0:AX * QR] + picked[AX * QR:]
                miss = jnp.sum(jnp.where(at_row, picked, 0.0), 0, keepdims=True) - value
                total = total + miss * miss
                eh, el = split(jnp.where(at_row, miss, 0.0))
                errors.append(jnp.concatenate([eh, el], 0))
            backs = [
                lax.dot_general(error, which, dims, preferred_element_type=jnp.float32)
                for error, which in zip(errors, whiches)
            ]
            for b, back in zip(blocks, backs):
                back = (0.5 / step_size) * (back[0:AX * QR] + back[AX * QR:])
                plus, minus = back[:, 0:HALF], back[:, HALF:]
                for a in range(AX):
                    spot = pl.multiple_of(a * NR + (2 * b + core) * QR, 8)
                    idle = pl.multiple_of(a * NR + (2 * b + 1 - core) * QR, 8)
                    own = slice(a * QR, (a + 1) * QR)
                    inject[k - 1, pl.ds(spot, QR), 0:HALF] = plus[own] + minus[own]
                    inject[k - 1, pl.ds(spot, QR), HALF:] = plus[own] - minus[own]
                    inject[k - 1, pl.ds(idle, QR), :] = jnp.zeros((QR, COEF), jnp.float32)
            return total

        for first_block in range(0, BLOCKS // 2, GROUP):
            msum[...] += group(first_block)

    for a in range(AX):
        for r in range(0, NR, CHUNK):
            store_split(a, r)
    forward_step(0)

    def onward(k, carry):
        forward_step(k)
        sample(k)
        return carry

    lax.fori_loop(1, STEPS, onward, 0)
    for a in range(AX):
        for r in range(0, NR, CHUNK):
            rows = slice(a * NR + r, a * NR + r + CHUNK)
            hist_u[0, rows, 0:HALF], hist_u[0, rows, HALF:] = expand_u(a, r)
    sample(STEPS)
    missed = jnp.broadcast_to(jnp.sum(msum[...], 1, keepdims=True), (8, NT))
    keep_out[QR:, :] = missed
    send_out[QR:, :] = missed

    mine = pl.multiple_of(me * QR, 8)
    for a in range(AX):
        spot = pl.multiple_of(a * NR + mine, 8)
        cos_part = state[pl.ds(spot, QR), 0:HALF]
        sin_part = state[pl.ds(spot, QR), HALF:]
        plain_c = cos_part * lane(4) + sin_part * lane(5)
        plain_s = pltpu.roll(cos_part * lane(6) + sin_part * lane(7), 63, 1)
        at_lane = lax.broadcasted_iota(jnp.int32, (QR, 128), 1)
        final_out[a, :, 0:128] = plain_c[:, 0:128]
        final_out[a, :, 128:256] = jnp.where(at_lane < 64, plain_c[:, 128:], plain_s[:, 0:128])
        final_out[a, :, 256:384] = plain_s[:, 128:]

    chip = pl.multiple_of((me - core) * QR, 16)

    def gather_gradient(k):
        wc = jnp.zeros((2 * QR, HALF), jnp.float32)
        ws = wc
        for a in range(AX):
            spot = pl.multiple_of(a * NR + chip, 16)
            wc = wc + (step_size * PROFILE[a]) * state[pl.ds(spot, 2 * QR), 0:HALF]
            ws = ws + (step_size * PROFILE[a]) * state[pl.ds(spot, 2 * QR), HALF:]
        gsum[:, 0:HALF] += turns[k, 4:5, :] * wc + turns[k, 5:6, :] * ws
        gsum[:, HALF:] += turns[k, 6:7, :] * wc + turns[k, 7:8, :] * ws

    for a in range(AX):
        for r in range(0, NR, CHUNK):
            rows = slice(a * NR + r, a * NR + r + CHUNK)
            eh, el = split(inject[STEPS - 1, rows, 0:HALF])
            oh, ol = split(inject[STEPS - 1, rows, HALF:])
            lc, ls = fold(mm3(eh, el, bch[0:HALF, :], bcl[0:HALF, :]), mm3(oh, ol, bsh[0:HALF, :], bsl[0:HALF, :]))
            state[rows, 0:HALF] = lc
            state[rows, HALF:] = ls
            store_split(a, r)

    def pull_back(k, a, rows, sw, eq, oq, coupled):
        eu, ou = hist_u[k, rows, 0:HALF], hist_u[k, rows, HALF:]
        ev, ov = hist_v[k, rows, 0:HALF], hist_v[k, rows, HALF:]
        speed_e = sw + advection_gain * eu
        speed_o = advection_gain * ou
        tve = -(speed_e * eq + speed_o * oq)
        tvo = -(speed_e * oq + speed_o * eq)
        eq = advection_gain * eq
        oq = advection_gain * oq
        tue = inject[k - 1, rows, 0:HALF] - (ev * eq + ov * oq)
        tuo = inject[k - 1, rows, HALF:] - (ev * oq + ov * eq)
        ueh, uel = split(tue)
        uoh, uol = split(tuo)
        veh, vel = split(tve)
        voh, vol = split(tvo)
        pc = mm3(ueh, uel, bch[0:HALF, :], bcl[0:HALF, :]) + mm3(voh, vol, bch[HALF:, :], bcl[HALF:, :])
        ps = mm3(uoh, uol, bsh[0:HALF, :], bsl[0:HALF, :]) + mm3(veh, vel, bsh[HALF:, :], bsl[HALF:, :])
        pc, ps = fold(pc, ps)
        new_c = decay * state[rows, 0:HALF] + pc + coupled[:, 0:HALF]
        new_s = decay * state[rows, HALF:] + ps + coupled[:, HALF:]
        if a < AX - 1:
            if isinstance(rows, slice):
                after = slice(rows.start + NR, rows.stop + NR)
            else:
                after = pl.ds(pl.multiple_of((a + 1) * NR + chip, 8), 2 * QR)
            new_c = new_c + reach * state[after, 0:HALF]
            new_s = new_s + reach * state[after, HALF:]
        state[rows, 0:HALF] = new_c
        state[rows, HALF:] = new_s

    def backward_step(k):
        couple(rtl)
        for a in range(AX):
            for r in range(0, NR, CHUNK):
                sw = jnp.concatenate([swirl[r:r + CHUNK, :], swirl[r:r + CHUNK, :]], 1)
                eq, oq = expand_u(a, r)
                pull_back(k, a, slice(a * NR + r, a * NR + r + CHUNK), sw, eq, oq, rad[a, r:r + CHUNK, :])
                store_split(a, r)

    def backward_chip():
        part = pl.ds(chip, 2 * QR)
        sw = jnp.concatenate([swirl[part, :], swirl[part, :]], 1)
        for a in range(AX):
            rows = pl.ds(pl.multiple_of(a * NR + chip, 16), 2 * QR)
            coupled = mm(rtl[part, :], high[a])
            ahead = high[a, part, :]
            rest = high[a, pl.ds(pl.multiple_of(2 * NR + chip, 16), 2 * QR), :]
            eq = mm3(ahead[:, 0:HALF], rest[:, 0:HALF], tch[:, 0:HALF], tcl[:, 0:HALF])
            oq = mm3(ahead[:, HALF:], rest[:, HALF:], tsh[:, 0:HALF], tsl[:, 0:HALF])
            pull_back(1, a, rows, sw, eq, oq, coupled)

    def inward(i, carry):
        k = STEPS - 1 - i
        gather_gradient(k)
        backward_step(k)
        return carry

    lax.fori_loop(0, STEPS - 2, inward, 0)
    gather_gradient(1)
    backward_chip()
    gather_gradient(0)
    gh, gl = split(gsum[...])
    gsum[...] = mm3(gh, gl, gth[...], gtl[...])
    keep_out[0:QR, :] = gsum[pl.ds(pl.multiple_of(core * QR, 8), QR), :]
    send_out[0:QR, :] = gsum[pl.ds(pl.multiple_of((1 - core) * QR, 8), QR), :]


def window_step(place, turns, radial_op, pieces):
    from_cos, from_sin = half_tables()
    whole = whole_table()
    tables = []
    for table in (from_cos, from_sin, 2.0 * step_size * from_cos.T, 2.0 * step_size * from_sin.T, whole.T, whole):
        tables += [jnp.asarray(part) for part in split_np(table)]
    operands = [place, turns, jnp.asarray(lane_rows()), radial_op, *tables, *pieces]
    vmem = pl.BlockSpec(memory_space=pltpu.VMEM)
    f32, bf16 = jnp.float32, jnp.bfloat16
    return pl.pallas_call(
        kernel,
        out_shape=(
            jax.ShapeDtypeStruct((AX, QR, 384), f32),
            jax.ShapeDtypeStruct((QR + 8, NT), f32),
            jax.ShapeDtypeStruct((QR + 8, NT), f32),
        ),
        in_specs=[pl.BlockSpec(memory_space=pltpu.SMEM)] + [vmem] * (len(operands) - 1),
        out_specs=(vmem, vmem, vmem),
        scratch_shapes=[
            pltpu.VMEM((ROWS, COEF), f32),
            pltpu.VMEM((AX, 3 * NR, COEF), bf16),
            pltpu.VMEM((AX, NR, COEF), f32),
            pltpu.VMEM((STEPS, ROWS, COEF), f32),
            pltpu.VMEM((STEPS, ROWS, COEF), f32),
            pltpu.VMEM((STEPS, ROWS, COEF), f32),
            pltpu.VMEM((NR, 3 * NR), bf16),
            pltpu.VMEM((NR, 3 * NR), bf16),
            pltpu.VMEM((NR, 128), f32),
            pltpu.VMEM((NR, COEF), f32),
            pltpu.VMEM((BLOCKS // 2 * STEPS, OBS), jnp.int32),
            pltpu.VMEM((BLOCKS // 2 * STEPS, OBS), f32),
            pltpu.VMEM((2 * QR, COEF), f32),
            pltpu.VMEM((1, OBS), f32),
        ],
        compiler_params=pltpu.CompilerParams(vmem_limit_bytes=VMEM_LIMIT),
    )(*operands)


def per_device(first_guess, forcing, swirl, radial_op, obs_index, obs_value, start_step):
    me = lax.axis_index("space")

    def space_swap(x, bits):
        return lax.ppermute(x, "space", [(i, i ^ bits) for i in range(BLOCKS)])

    def space_turn(x, d):
        return lax.ppermute(x, "space", [(i, i // 8 * 8 + (i + 2 * d) % 8) for i in range(BLOCKS)])

    def win_send(x, where):
        return lax.ppermute(x, "win", [(i, where(i)) for i in range(16)])

    extra = jnp.concatenate(
        [
            obs_index[0].astype(jnp.float32),
            obs_value[0],
            jnp.pad(swirl[None, :], ((0, 7), (0, OBS - QR))),
        ],
        0,
    )
    message = jnp.concatenate([first_guess[0, 0], first_guess[0, 1], forcing, extra], 1)
    other_x = space_swap(message, 8)
    both = jnp.concatenate([message, other_x], 0)
    turned = [space_turn(both, d) for d in (1, 2, 3)]
    pieces = list(lax.optimization_barrier((message, other_x, *turned)))
    pieces += [space_swap(piece, 1) for piece in pieces]

    turns = turn_tables(start_step[0])
    final, keep, send = window_step(me.astype(jnp.int32).reshape(1), turns, radial_op, pieces)

    both_cores = keep + space_swap(send, 1)
    misfit = both_cores[QR, 0:1] * (0.5 / (STEPS * BLOCKS * OBS))
    total = both_cores[0:QR]
    near = [win_send(total, lambda i, f=f: i ^ f) for f in (1, 2, 3)]
    total = total + near[0] + near[1] + near[2]
    far = [win_send(total, lambda i, d=d: (i + 2 * d) % 16) for d in (2, 4, 6)]
    total = total + far[0] + far[1] + far[2]
    return final[None], misfit, total


def solution(mesh):
    return jax.shard_map(
        per_device,
        mesh=mesh,
        in_specs=(
            P("win", None, "space", None),
            P("space", None),
            P("space"),
            P(),
            P("win", None, "space"),
            P("win", None, "space"),
            P("win"),
        ),
        out_specs=(P("win", None, "space", None), P("win"), P("space", None)),
        check_vma=False,
    )
```

```python
import math

import jax
import jax.numpy as jnp
import ml_dtypes
import numpy as np
from jax import lax
from jax.experimental import pallas as pl
from jax.experimental.pallas import tpu as pltpu
from jax.sharding import PartitionSpec as P

MODES = 192
STEPS = 8
ROT = 8
NT = 512
NR = 384
AX = 2
HALF = NT // 2
BLOCKS = 16
QR = NR // BLOCKS
OBS = 256
ROWS = AX * NR
COEF = 2 * HALF
GROUP = 8
CHUNK = 384
VMEM_LIMIT = 60 * 1024 * 1024

step_size = 0.25
radial_scale = 0.4
radial_damping = 0.4
axial_speed = 0.4
advection_gain = 0.2
PROFILE = [math.exp(-(((a + 0.5 - AX / 2.0) * (4.0 / AX)) ** 2)) for a in range(AX)]

OMEGA = 2.0 * math.pi / NT
PHI = OMEGA * np.arange(HALF) / 2.0


def split_np(table):
    high = table.astype(ml_dtypes.bfloat16)
    low = (table - high.astype(np.float64)).astype(ml_dtypes.bfloat16)
    return high, low


def half_tables():
    m = np.arange(HALF)[:, None].astype(np.float64)
    theta = np.arange(HALF)[None, :] + 0.5
    norm = np.where(m == 0, 1.0 / math.sqrt(NT), math.sqrt(2.0 / NT))
    cosine = norm * np.cos(OMEGA * m * theta)
    sine = norm * np.sin(OMEGA * m * theta)
    slope = OMEGA * m
    kept = m < MODES
    last = m == MODES
    sin_phi, cos_phi = math.sin(PHI[MODES]), math.cos(PHI[MODES])
    even_u = np.where(kept, cosine, np.where(last, -sin_phi * cosine, 0.0))
    odd_u = np.where(kept & (m > 0), sine, np.where(last, cos_phi * sine, 0.0))
    odd_v = np.where(kept, -slope * sine, np.where(last, sin_phi * slope * sine, 0.0))
    even_v = np.where(kept & (m > 0), slope * cosine, np.where(last, cos_phi * slope * cosine, 0.0))
    from_cos = np.concatenate([even_u, odd_v], 1)
    from_sin = np.concatenate([odd_u, even_v], 1)
    return from_cos, from_sin


def whole_table():
    m = np.arange(HALF)[:, None].astype(np.float64)
    theta = np.arange(NT)[None, :] + 0.5
    norm = np.where(m == 0, 1.0 / math.sqrt(NT), math.sqrt(2.0 / NT))
    cosine = np.where(m <= MODES, norm * np.cos(OMEGA * m * theta), 0.0)
    sine = np.where((m <= MODES) & (m > 0), norm * np.sin(OMEGA * m * theta), 0.0)
    return np.concatenate([cosine, sine], 0)


def lane_rows():
    m = np.arange(HALF)
    kept = (m >= 1) & (m < MODES)
    last = m == MODES
    cos_phi, sin_phi = np.cos(PHI), np.sin(PHI)
    rows = np.zeros((16, HALF))
    rows[0] = np.where(kept, cos_phi, np.where(m == 0, 1.0, 0.0))
    rows[1] = np.where(kept, -sin_phi, np.where(last, 1.0, 0.0))
    rows[2] = np.where(kept, sin_phi, 0.0)
    rows[3] = np.where(kept, cos_phi, np.where(last, 1.0, 0.0))
    rows[4] = np.where(kept, cos_phi, np.where(m == 0, 1.0, 0.0))
    rows[5] = np.where(kept, sin_phi, 0.0)
    rows[6] = np.where(kept, -sin_phi, 0.0)
    rows[7] = np.where(kept, cos_phi, np.where(last, 1.0, 0.0))
    rows[8] = np.where(m <= MODES, 1.0 - step_size * (radial_damping + axial_speed + (m / MODES) ** 2), 0.0)
    rows[9] = np.where(last, 1.0, 0.0)
    return rows.astype(np.float32)


def turn_tables(phase_start):
    m = jnp.arange(HALF, dtype=jnp.int32)[None, :]
    cells = ROT * (phase_start + jnp.arange(STEPS, dtype=jnp.int32))[:, None]
    angles = OMEGA * ((m * cells) % NT).astype(jnp.float32)
    cosine, sine = jnp.cos(angles), jnp.sin(angles)
    sin_phi, cos_phi = math.sin(PHI[MODES]), math.cos(PHI[MODES])
    last = m == MODES
    first = -sin_phi * cosine + cos_phi * sine
    second = sin_phi * sine + cos_phi * cosine
    forward = [
        jnp.where(last, first, cosine),
        jnp.where(last, second, -sine),
        jnp.where(last, first, sine),
        jnp.where(last, second, cosine),
    ]
    back = [
        forward[0],
        jnp.where(last, 0.0, sine),
        forward[1],
        jnp.where(last, 0.0, cosine),
    ]
    keep = (m <= MODES).astype(jnp.float32)
    return jnp.stack([row * keep for row in forward + back], 1)


def split(x):
    high = x.astype(jnp.bfloat16)
    return high, (x - high.astype(jnp.float32)).astype(jnp.bfloat16)


def mm(a, b):
    return jnp.dot(a, b, preferred_element_type=jnp.float32)


def mm3(xh, xl, th, tl):
    return mm(xh, th) + mm(xl, th) + mm(xh, tl)


def kernel(
    place, turns, lanes, radial_op, tch, tcl, tsh, tsl, bch, bcl, bsh, bsl, fth, ftl, gth, gtl,
    p0, p1, p2, p3, p4, p5, q0, q1, q2, q3, q4, q5,
    final_out, keep_out, send_out,
    state, high, rad, hist_u, hist_v, inject, rl, rtl, swirl, forced, obs_i, obs_v, gsum, msum,
):
    me = place[0]
    core = me % 2
    across = me // 8
    up = (me // 2) % 4

    def block_of(d, flip_x, flip_core):
        y = (up + 4 - d) % 4
        x = 1 - across if flip_x else across
        c = 1 - core if flip_core else core
        return x * 8 + y * 2 + c

    sources = [(p0, 0, 0, False, False), (p1, 0, 0, True, False), (q0, 0, 0, False, True), (q1, 0, 0, True, True)]
    for d, pd, qd in ((1, p2, q2), (3, p3, q3)):
        sources += [(pd, 0, d, False, False), (pd, QR, d, True, False), (qd, 0, d, False, True), (qd, QR, d, True, True)]
    sources += [(p4, 0, 2, False, False), (p5, 0, 2, True, False), (q4, 0, 2, False, True), (q5, 0, 2, True, True)]

    def lane(i):
        return lanes[i:i + 1, :]

    square = lax.broadcasted_iota(jnp.int32, (QR, 128), 0) == lax.broadcasted_iota(jnp.int32, (QR, 128), 1)
    for ref, row, d, flip_x, flip_core in sources:
        block = block_of(d, flip_x, flip_core)
        at = pl.multiple_of(block * QR, 8)
        for a in range(AX):
            first = ref[row:row + QR, 384 * a:384 * a + HALF]
            second = pltpu.roll(ref[row:row + QR, 384 * a + 128:384 * a + 384], 193, 1)
            spot = pl.multiple_of(a * NR + at, 8)
            state[pl.ds(spot, QR), 0:HALF] = first * lane(0) + second * lane(1)
            state[pl.ds(spot, QR), HALF:COEF] = first * lane(2) + second * lane(3)
        forced[pl.ds(at, QR), :] = ref[row:row + QR, 768:1280]
        spread = jnp.where(square, ref[row + 16:row + 17, 1280:1408], 0.0)
        swirl[pl.ds(at, QR), :] = jnp.broadcast_to(jnp.sum(spread, 1, keepdims=True), (QR, 128))
        if not flip_core:
            slot = pl.multiple_of((block // 2) * STEPS, 8)
            obs_i[pl.ds(slot, STEPS), :] = ref[row:row + 8, 1280:1536].astype(jnp.int32)
            obs_v[pl.ds(slot, STEPS), :] = ref[row + 8:row + 16, 1280:1536]

    fh, fl = split(forced[...])
    forced[...] = mm3(fh, fl, fth[...], ftl[...]) * step_size

    scaled = (step_size * radial_scale) * radial_op[...]
    rh, rlow = split(scaled)
    rl[:, 0:NR], rl[:, NR:2 * NR], rl[:, 2 * NR:] = rh, rlow, rh
    th, tlow = split(scaled.T)
    rtl[:, 0:NR], rtl[:, NR:2 * NR], rtl[:, 2 * NR:] = th, tlow, th
    gsum[...] = jnp.zeros_like(gsum)
    msum[...] = jnp.zeros_like(msum)

    mark = lane(9)
    decay = lane(8)
    reach = step_size * axial_speed

    def store_split(a, r):
        h, l = split(state[a * NR + r:a * NR + r + CHUNK, :])
        high[a, r:r + CHUNK, :] = h
        high[a, NR + r:NR + r + CHUNK, :] = h
        high[a, 2 * NR + r:2 * NR + r + CHUNK, :] = l

    def couple(operator):
        for a in range(AX):
            rad[a] = mm(operator[...], high[a])

    def halves(a, r, part):
        lanes_of = slice(0, HALF) if part == 0 else slice(HALF, COEF)
        return high[a, r:r + CHUNK, lanes_of], high[a, 2 * NR + r:2 * NR + r + CHUNK, lanes_of]

    def fold(pc, ps):
        return pc + mark * ps, ps + mark * pc

    def expand_u(a, r):
        ch, cl = halves(a, r, 0)
        sh, sl = halves(a, r, 1)
        eu = mm3(ch, cl, tch[:, 0:HALF], tcl[:, 0:HALF])
        ou = mm3(sh, sl, tsh[:, 0:HALF], tsl[:, 0:HALF])
        return eu, ou

    def slot_v(k):
        return (k + STEPS - 2) % (STEPS - 1)

    def forward_step(k):
        expanded = [None, None]
        fields = [None, None]
        for a in range(AX - 1, -1, -1):
            ch, cl = halves(a, 0, 0)
            sh, sl = halves(a, 0, 1)
            expanded[a] = (mm3(ch, cl, tch[...], tcl[...]), mm3(sh, sl, tsh[...], tsl[...]))
        sw = jnp.concatenate([swirl[...], swirl[...]], 1)
        for a in range(AX - 1, -1, -1):
            rows = slice(a * NR, (a + 1) * NR)
            from_cos, from_sin = expanded[a]
            eu, ov = from_cos[:, 0:HALF], from_cos[:, HALF:]
            ou, ev = from_sin[:, 0:HALF], from_sin[:, HALF:]
            hist_u[k, rows, 0:HALF] = eu
            hist_u[k, rows, HALF:] = ou
            hist_v[slot_v(k), rows, 0:HALF] = ev
            hist_v[slot_v(k), rows, HALF:] = ov
            speed_e = sw + advection_gain * eu
            speed_o = advection_gain * ou
            fields[a] = split(-(speed_e * ev + speed_o * ov)) + split(-(speed_e * ov + speed_o * ev))
            rad[a] = mm(rl[...], high[a])
        for a in range(AX - 1, -1, -1):
            rows = slice(a * NR, (a + 1) * NR)
            geh, gel, goh, gol = fields[a]
            pc, ps = fold(mm3(geh, gel, bch[0:HALF, :], bcl[0:HALF, :]), mm3(goh, gol, bsh[0:HALF, :], bsl[0:HALF, :]))
            force_c, force_s = forced[:, 0:HALF], forced[:, HALF:COEF]
            body_c = turns[k, 0:1, :] * force_c + turns[k, 1:2, :] * force_s
            body_s = turns[k, 2:3, :] * force_c + turns[k, 3:4, :] * force_s
            new_c = decay * state[rows, 0:HALF] + pc + PROFILE[a] * body_c + rad[a, :, 0:HALF]
            new_s = decay * state[rows, HALF:] + ps + PROFILE[a] * body_s + rad[a, :, HALF:]
            if a > 0:
                before = slice(rows.start - NR, rows.stop - NR)
                new_c = new_c + reach * state[before, 0:HALF]
                new_s = new_s + reach * state[before, HALF:]
            state[rows, 0:HALF] = new_c
            state[rows, HALF:] = new_s
            store_split(a, 0)

    tall = lax.broadcasted_iota(jnp.int32, (HALF, OBS), 0).astype(jnp.float32).astype(jnp.bfloat16)
    short = lax.broadcasted_iota(jnp.int32, (AX * QR, OBS), 0)
    one_wide = jnp.ones((HALF, OBS), jnp.bfloat16)
    zero_wide = jnp.zeros((HALF, OBS), jnp.bfloat16)

    def sample(k):
        held = k % STEPS

        dims = (((1,), (1,)), ((), ()))

        def group(first_block):
            blocks = range(first_block, first_block + GROUP)
            ats, values, whiches, picks = [], [], [], []
            for b in blocks:
                block = 2 * b + core
                cell = obs_i[pl.ds(b * STEPS + k - 1, 1), :]
                values.append(obs_v[pl.ds(b * STEPS + k - 1, 1), :])
                column = cell & (NT - 1)
                in_first = column < HALF
                first = jnp.where(in_first, column, -1).astype(jnp.float32).astype(jnp.bfloat16)
                second = jnp.where(in_first, -1, NT - 1 - column).astype(jnp.float32).astype(jnp.bfloat16)
                which = jnp.concatenate(
                    [jnp.where(tall == first, one_wide, zero_wide), jnp.where(tall == second, one_wide, zero_wide)], 0
                )
                whiches.append(which)
                ats.append(short == (cell >> 9))
                parts = []
                for a in range(AX):
                    spot = pl.multiple_of(a * NR + block * QR, 8)
                    eu = hist_u[held, pl.ds(spot, QR), 0:HALF]
                    ou = hist_u[held, pl.ds(spot, QR), HALF:]
                    parts.append(jnp.concatenate([eu + ou, eu - ou], 1))
                uh, ul = split(jnp.concatenate(parts, 0))
                picks.append(mm(jnp.concatenate([uh, ul], 0), which))
            errors, total = [], 0.0
            for at_row, value, picked in zip(ats, values, picks):
                picked = picked[0:AX * QR] + picked[AX * QR:]
                miss = jnp.sum(jnp.where(at_row, picked, 0.0), 0, keepdims=True) - value
                total = total + miss * miss
                eh, el = split(jnp.where(at_row, miss, 0.0))
                errors.append(jnp.concatenate([eh, el], 0))
            backs = [
                lax.dot_general(error, which, dims, preferred_element_type=jnp.float32)
                for error, which in zip(errors, whiches)
            ]
            for b, back in zip(blocks, backs):
                back = (0.5 / step_size) * (back[0:AX * QR] + back[AX * QR:])
                plus, minus = back[:, 0:HALF], back[:, HALF:]
                for a in range(AX):
                    spot = pl.multiple_of(a * NR + (2 * b + core) * QR, 8)
                    idle = pl.multiple_of(a * NR + (2 * b + 1 - core) * QR, 8)
                    own = slice(a * QR, (a + 1) * QR)
                    inject[k - 1, pl.ds(spot, QR), 0:HALF] = plus[own] + minus[own]
                    inject[k - 1, pl.ds(spot, QR), HALF:] = plus[own] - minus[own]
                    inject[k - 1, pl.ds(idle, QR), :] = jnp.zeros((QR, COEF), jnp.float32)
            return total

        for first_block in range(0, BLOCKS // 2, GROUP):
            msum[...] += group(first_block)

    for a in range(AX):
        for r in range(0, NR, CHUNK):
            store_split(a, r)
    forward_step(0)

    def onward(k, carry):
        forward_step(k)
        sample(k)
        return carry

    lax.fori_loop(1, STEPS, onward, 0)
    for a in range(AX):
        for r in range(0, NR, CHUNK):
            rows = slice(a * NR + r, a * NR + r + CHUNK)
            hist_u[0, rows, 0:HALF], hist_u[0, rows, HALF:] = expand_u(a, r)
    sample(STEPS)
    missed = jnp.broadcast_to(jnp.sum(msum[...], 1, keepdims=True), (8, NT))
    keep_out[QR:, :] = missed
    send_out[QR:, :] = missed

    mine = pl.multiple_of(me * QR, 8)
    for a in range(AX):
        spot = pl.multiple_of(a * NR + mine, 8)
        cos_part = state[pl.ds(spot, QR), 0:HALF]
        sin_part = state[pl.ds(spot, QR), HALF:]
        plain_c = cos_part * lane(4) + sin_part * lane(5)
        plain_s = pltpu.roll(cos_part * lane(6) + sin_part * lane(7), 63, 1)
        at_lane = lax.broadcasted_iota(jnp.int32, (QR, 128), 1)
        final_out[a, :, 0:128] = plain_c[:, 0:128]
        final_out[a, :, 128:256] = jnp.where(at_lane < 64, plain_c[:, 128:], plain_s[:, 0:128])
        final_out[a, :, 256:384] = plain_s[:, 128:]

    chip = pl.multiple_of((me - core) * QR, 16)

    def gather_gradient(k):
        wc = jnp.zeros((2 * QR, HALF), jnp.float32)
        ws = wc
        for a in range(AX):
            spot = pl.multiple_of(a * NR + chip, 16)
            wc = wc + (step_size * PROFILE[a]) * state[pl.ds(spot, 2 * QR), 0:HALF]
            ws = ws + (step_size * PROFILE[a]) * state[pl.ds(spot, 2 * QR), HALF:]
        gsum[:, 0:HALF] += turns[k, 4:5, :] * wc + turns[k, 5:6, :] * ws
        gsum[:, HALF:] += turns[k, 6:7, :] * wc + turns[k, 7:8, :] * ws

    for a in range(AX):
        for r in range(0, NR, CHUNK):
            rows = slice(a * NR + r, a * NR + r + CHUNK)
            eh, el = split(inject[STEPS - 1, rows, 0:HALF])
            oh, ol = split(inject[STEPS - 1, rows, HALF:])
            lc, ls = fold(mm3(eh, el, bch[0:HALF, :], bcl[0:HALF, :]), mm3(oh, ol, bsh[0:HALF, :], bsl[0:HALF, :]))
            state[rows, 0:HALF] = lc
            state[rows, HALF:] = ls
            store_split(a, r)

    def pull_back(k, a, rows, sw, eq, oq, coupled):
        gather_back(a, rows, weigh(k, rows, sw, eq, oq), coupled)

    def weigh(k, rows, sw, eq, oq):
        eu, ou = hist_u[k, rows, 0:HALF], hist_u[k, rows, HALF:]
        ev, ov = hist_v[slot_v(k), rows, 0:HALF], hist_v[slot_v(k), rows, HALF:]
        speed_e = sw + advection_gain * eu
        speed_o = advection_gain * ou
        tve = -(speed_e * eq + speed_o * oq)
        tvo = -(speed_e * oq + speed_o * eq)
        eq = advection_gain * eq
        oq = advection_gain * oq
        tue = inject[k - 1, rows, 0:HALF] - (ev * eq + ov * oq)
        tuo = inject[k - 1, rows, HALF:] - (ev * oq + ov * eq)
        return split(tue) + split(tuo) + split(tve) + split(tvo)

    def gather_back(a, rows, fields, coupled):
        ueh, uel, uoh, uol, veh, vel, voh, vol = fields
        pc = mm3(ueh, uel, bch[0:HALF, :], bcl[0:HALF, :]) + mm3(voh, vol, bch[HALF:, :], bcl[HALF:, :])
        ps = mm3(uoh, uol, bsh[0:HALF, :], bsl[0:HALF, :]) + mm3(veh, vel, bsh[HALF:, :], bsl[HALF:, :])
        pc, ps = fold(pc, ps)
        new_c = decay * state[rows, 0:HALF] + pc + coupled[:, 0:HALF]
        new_s = decay * state[rows, HALF:] + ps + coupled[:, HALF:]
        if a < AX - 1:
            if isinstance(rows, slice):
                after = slice(rows.start + NR, rows.stop + NR)
            else:
                after = pl.ds(pl.multiple_of((a + 1) * NR + chip, 8), 2 * QR)
            new_c = new_c + reach * state[after, 0:HALF]
            new_s = new_s + reach * state[after, HALF:]
        state[rows, 0:HALF] = new_c
        state[rows, HALF:] = new_s

    def backward_step(k):
        synthesized = [expand_u(a, 0) for a in range(AX)]
        sw = jnp.concatenate([swirl[...], swirl[...]], 1)
        fields = []
        for a in range(AX):
            rows = slice(a * NR, (a + 1) * NR)
            fields.append(weigh(k, rows, sw, *synthesized[a]))
            rad[a] = mm(rtl[...], high[a])
        for a in range(AX):
            rows = slice(a * NR, (a + 1) * NR)
            gather_back(a, rows, fields[a], rad[a])
            store_split(a, 0)

    def backward_chip():
        part = pl.ds(chip, 2 * QR)
        sw = jnp.concatenate([swirl[part, :], swirl[part, :]], 1)
        for a in range(AX):
            rows = pl.ds(pl.multiple_of(a * NR + chip, 16), 2 * QR)
            coupled = mm(rtl[part, :], high[a])
            ahead = high[a, part, :]
            rest = high[a, pl.ds(pl.multiple_of(2 * NR + chip, 16), 2 * QR), :]
            eq = mm3(ahead[:, 0:HALF], rest[:, 0:HALF], tch[:, 0:HALF], tcl[:, 0:HALF])
            oq = mm3(ahead[:, HALF:], rest[:, HALF:], tsh[:, 0:HALF], tsl[:, 0:HALF])
            pull_back(1, a, rows, sw, eq, oq, coupled)

    def inward(i, carry):
        k = STEPS - 1 - i
        gather_gradient(k)
        backward_step(k)
        return carry

    lax.fori_loop(0, STEPS - 2, inward, 0)
    gather_gradient(1)
    backward_chip()
    gather_gradient(0)
    gh, gl = split(gsum[...])
    gsum[...] = mm3(gh, gl, gth[...], gtl[...])
    keep_out[0:QR, :] = gsum[pl.ds(pl.multiple_of(core * QR, 8), QR), :]
    send_out[0:QR, :] = gsum[pl.ds(pl.multiple_of((1 - core) * QR, 8), QR), :]


def window_step(place, turns, radial_op, pieces):
    from_cos, from_sin = half_tables()
    whole = whole_table()
    tables = []
    for table in (from_cos, from_sin, 2.0 * step_size * from_cos.T, 2.0 * step_size * from_sin.T, whole.T, whole):
        tables += [jnp.asarray(part) for part in split_np(table)]
    operands = [place, turns, jnp.asarray(lane_rows()), radial_op, *tables, *pieces]
    vmem = pl.BlockSpec(memory_space=pltpu.VMEM)
    f32, bf16 = jnp.float32, jnp.bfloat16
    return pl.pallas_call(
        kernel,
        out_shape=(
            jax.ShapeDtypeStruct((AX, QR, 384), f32),
            jax.ShapeDtypeStruct((QR + 8, NT), f32),
            jax.ShapeDtypeStruct((QR + 8, NT), f32),
        ),
        in_specs=[pl.BlockSpec(memory_space=pltpu.SMEM)] + [vmem] * (len(operands) - 1),
        out_specs=(vmem, vmem, vmem),
        scratch_shapes=[
            pltpu.VMEM((ROWS, COEF), f32),
            pltpu.VMEM((AX, 3 * NR, COEF), bf16),
            pltpu.VMEM((AX, NR, COEF), f32),
            pltpu.VMEM((STEPS, ROWS, COEF), f32),
            pltpu.VMEM((STEPS - 1, ROWS, COEF), f32),
            pltpu.VMEM((STEPS, ROWS, COEF), f32),
            pltpu.VMEM((NR, 3 * NR), bf16),
            pltpu.VMEM((NR, 3 * NR), bf16),
            pltpu.VMEM((NR, 128), f32),
            pltpu.VMEM((NR, COEF), f32),
            pltpu.VMEM((BLOCKS // 2 * STEPS, OBS), jnp.int32),
            pltpu.VMEM((BLOCKS // 2 * STEPS, OBS), f32),
            pltpu.VMEM((2 * QR, COEF), f32),
            pltpu.VMEM((1, OBS), f32),
        ],
        compiler_params=pltpu.CompilerParams(vmem_limit_bytes=VMEM_LIMIT),
    )(*operands)


def per_device(first_guess, forcing, swirl, radial_op, obs_index, obs_value, start_step):
    me = lax.axis_index("space")

    def space_swap(x, bits):
        return lax.ppermute(x, "space", [(i, i ^ bits) for i in range(BLOCKS)])

    def space_turn(x, d):
        return lax.ppermute(x, "space", [(i, i // 8 * 8 + (i + 2 * d) % 8) for i in range(BLOCKS)])

    def win_send(x, where):
        return lax.ppermute(x, "win", [(i, where(i)) for i in range(16)])

    extra = jnp.concatenate(
        [
            obs_index[0].astype(jnp.float32),
            obs_value[0],
            jnp.pad(swirl[None, :], ((0, 7), (0, OBS - QR))),
        ],
        0,
    )
    message = jnp.concatenate([first_guess[0, 0], first_guess[0, 1], forcing, extra], 1)
    other_x = space_swap(message, 8)
    both = jnp.concatenate([message, other_x], 0)
    left, right = space_turn(both, 1), space_turn(both, 3)
    message, other_x, left, right, ahead, behind = lax.optimization_barrier(
        (message, other_x, left, right, left[:QR], right[QR:])
    )
    opposite = [space_turn(ahead, 1), space_turn(behind, 3)]
    near_pieces = [message, other_x, left, right]
    swapped = [space_swap(piece, 1) for piece in near_pieces]
    opposite, swapped = lax.optimization_barrier((opposite, swapped))
    pieces = near_pieces + opposite + swapped + [space_swap(piece, 1) for piece in opposite]

    turns = turn_tables(start_step[0])
    final, keep, send = window_step(me.astype(jnp.int32).reshape(1), turns, radial_op, pieces)

    both_cores = keep + space_swap(send, 1)
    misfit = both_cores[QR, 0:1] * (0.5 / (STEPS * BLOCKS * OBS))
    total = both_cores[0:QR]
    near = [win_send(total, lambda i, f=f: i ^ f) for f in (1, 2, 3)]
    total = total + near[0] + near[1] + near[2]
    far = [win_send(total, lambda i, d=d: (i + 2 * d) % 16) for d in (2, 4, 6)]
    total = total + far[0] + far[1] + far[2]
    return final[None], misfit, total


def solution(mesh):
    return jax.shard_map(
        per_device,
        mesh=mesh,
        in_specs=(
            P("win", None, "space", None),
            P("space", None),
            P("space"),
            P(),
            P("win", None, "space"),
            P("win", None, "space"),
            P("win"),
        ),
        out_specs=(P("win", None, "space", None), P("win"), P("space", None)),
        check_vma=False,
    )
```

```python
import math

import jax
import jax.numpy as jnp
import ml_dtypes
import numpy as np
from jax import lax
from jax.experimental import pallas as pl
from jax.experimental.pallas import tpu as pltpu
from jax.sharding import PartitionSpec as P

MODES = 192
STEPS = 8
ROT = 8
NT = 512
NR = 384
AX = 2
HALF = NT // 2
BLOCKS = 16
QR = NR // BLOCKS
OBS = 256
ROWS = AX * NR
COEF = 2 * HALF
GROUP = 8
CHUNK = 384
VMEM_LIMIT = 60 * 1024 * 1024

step_size = 0.25
radial_scale = 0.4
radial_damping = 0.4
axial_speed = 0.4
advection_gain = 0.2
PROFILE = [math.exp(-(((a + 0.5 - AX / 2.0) * (4.0 / AX)) ** 2)) for a in range(AX)]

OMEGA = 2.0 * math.pi / NT
PHI = OMEGA * np.arange(HALF) / 2.0


def split_np(table):
    high = table.astype(ml_dtypes.bfloat16)
    low = (table - high.astype(np.float64)).astype(ml_dtypes.bfloat16)
    return high, low


def half_tables():
    m = np.arange(HALF)[:, None].astype(np.float64)
    theta = np.arange(HALF)[None, :] + 0.5
    norm = np.where(m == 0, 1.0 / math.sqrt(NT), math.sqrt(2.0 / NT))
    cosine = norm * np.cos(OMEGA * m * theta)
    sine = norm * np.sin(OMEGA * m * theta)
    slope = OMEGA * m
    kept = m < MODES
    last = m == MODES
    sin_phi, cos_phi = math.sin(PHI[MODES]), math.cos(PHI[MODES])
    even_u = np.where(kept, cosine, np.where(last, -sin_phi * cosine, 0.0))
    odd_u = np.where(kept & (m > 0), sine, np.where(last, cos_phi * sine, 0.0))
    odd_v = np.where(kept, -slope * sine, np.where(last, sin_phi * slope * sine, 0.0))
    even_v = np.where(kept & (m > 0), slope * cosine, np.where(last, cos_phi * slope * cosine, 0.0))
    from_cos = np.concatenate([even_u, odd_v], 1)
    from_sin = np.concatenate([odd_u, even_v], 1)
    return from_cos, from_sin


def whole_table():
    m = np.arange(HALF)[:, None].astype(np.float64)
    theta = np.arange(NT)[None, :] + 0.5
    norm = np.where(m == 0, 1.0 / math.sqrt(NT), math.sqrt(2.0 / NT))
    cosine = np.where(m <= MODES, norm * np.cos(OMEGA * m * theta), 0.0)
    sine = np.where((m <= MODES) & (m > 0), norm * np.sin(OMEGA * m * theta), 0.0)
    return np.concatenate([cosine, sine], 0)


def lane_rows():
    m = np.arange(HALF)
    kept = (m >= 1) & (m < MODES)
    last = m == MODES
    cos_phi, sin_phi = np.cos(PHI), np.sin(PHI)
    rows = np.zeros((16, HALF))
    rows[0] = np.where(kept, cos_phi, np.where(m == 0, 1.0, 0.0))
    rows[1] = np.where(kept, -sin_phi, np.where(last, 1.0, 0.0))
    rows[2] = np.where(kept, sin_phi, 0.0)
    rows[3] = np.where(kept, cos_phi, np.where(last, 1.0, 0.0))
    rows[4] = np.where(kept, cos_phi, np.where(m == 0, 1.0, 0.0))
    rows[5] = np.where(kept, sin_phi, 0.0)
    rows[6] = np.where(kept, -sin_phi, 0.0)
    rows[7] = np.where(kept, cos_phi, np.where(last, 1.0, 0.0))
    rows[8] = np.where(m <= MODES, 1.0 - step_size * (radial_damping + axial_speed + (m / MODES) ** 2), 0.0)
    rows[9] = np.where(last, 1.0, 0.0)
    return rows.astype(np.float32)


def turn_tables(phase_start):
    m = jnp.arange(HALF, dtype=jnp.int32)[None, :]
    cells = ROT * (phase_start + jnp.arange(STEPS, dtype=jnp.int32))[:, None]
    angles = OMEGA * ((m * cells) % NT).astype(jnp.float32)
    cosine, sine = jnp.cos(angles), jnp.sin(angles)
    sin_phi, cos_phi = math.sin(PHI[MODES]), math.cos(PHI[MODES])
    last = m == MODES
    first = -sin_phi * cosine + cos_phi * sine
    second = sin_phi * sine + cos_phi * cosine
    forward = [
        jnp.where(last, first, cosine),
        jnp.where(last, second, -sine),
        jnp.where(last, first, sine),
        jnp.where(last, second, cosine),
    ]
    back = [
        forward[0],
        jnp.where(last, 0.0, sine),
        forward[1],
        jnp.where(last, 0.0, cosine),
    ]
    keep = (m <= MODES).astype(jnp.float32)
    return jnp.stack([row * keep for row in forward + back], 1)


def split(x):
    high = x.astype(jnp.bfloat16)
    return high, (x - high.astype(jnp.float32)).astype(jnp.bfloat16)


def mm(a, b):
    return jnp.dot(a, b, preferred_element_type=jnp.float32)


def mm3(xh, xl, th, tl):
    return mm(xh, th) + mm(xl, th) + mm(xh, tl)


def kernel(
    place, turns, lanes, radial_op, tch, tcl, tsh, tsl, bch, bcl, bsh, bsl, fth, ftl, gth, gtl,
    p0, p1, p2, p3, p4, p5, q0, q1, q2, q3, q4, q5,
    final_out, keep_out, send_out,
    state, high, rad, hist_u, hist_v, inject, rl, rtl, swirl, forced, obs_i, obs_v, gsum, msum,
):
    me = place[0]
    core = me % 2
    across = me // 8
    up = (me // 2) % 4

    def block_of(d, flip_x, flip_core):
        y = (up + 4 - d) % 4
        x = 1 - across if flip_x else across
        c = 1 - core if flip_core else core
        return x * 8 + y * 2 + c

    sources = [(p0, 0, 0, False, False), (p1, 0, 0, True, False), (q0, 0, 0, False, True), (q1, 0, 0, True, True)]
    for d, pd, qd in ((1, p2, q2), (3, p3, q3)):
        sources += [(pd, 0, d, False, False), (pd, QR, d, True, False), (qd, 0, d, False, True), (qd, QR, d, True, True)]
    sources += [(p4, 0, 2, False, False), (p5, 0, 2, True, False), (q4, 0, 2, False, True), (q5, 0, 2, True, True)]

    def lane(i):
        return lanes[i:i + 1, :]

    square = lax.broadcasted_iota(jnp.int32, (QR, 128), 0) == lax.broadcasted_iota(jnp.int32, (QR, 128), 1)
    for ref, row, d, flip_x, flip_core in sources:
        block = block_of(d, flip_x, flip_core)
        at = pl.multiple_of(block * QR, 8)
        for a in range(AX):
            first = ref[row:row + QR, 384 * a:384 * a + HALF]
            second = pltpu.roll(ref[row:row + QR, 384 * a + 128:384 * a + 384], 193, 1)
            spot = pl.multiple_of(a * NR + at, 8)
            state[pl.ds(spot, QR), 0:HALF] = first * lane(0) + second * lane(1)
            state[pl.ds(spot, QR), HALF:COEF] = first * lane(2) + second * lane(3)
        forced[pl.ds(at, QR), :] = ref[row:row + QR, 768:1280]
        spread = jnp.where(square, ref[row + 16:row + 17, 1280:1408], 0.0)
        swirl[pl.ds(at, QR), :] = jnp.broadcast_to(jnp.sum(spread, 1, keepdims=True), (QR, 128))
        if not flip_core:
            slot = pl.multiple_of((block // 2) * STEPS, 8)
            obs_i[pl.ds(slot, STEPS), :] = ref[row:row + 8, 1280:1536].astype(jnp.int32)
            obs_v[pl.ds(slot, STEPS), :] = ref[row + 8:row + 16, 1280:1536]

    fh, fl = split(forced[...])
    forced[...] = mm3(fh, fl, fth[...], ftl[...]) * step_size

    scaled = (step_size * radial_scale) * radial_op[...]
    rh, rlow = split(scaled)
    rl[:, 0:NR], rl[:, NR:2 * NR], rl[:, 2 * NR:] = rh, rlow, rh
    th, tlow = split(scaled.T)
    rtl[:, 0:NR], rtl[:, NR:2 * NR], rtl[:, 2 * NR:] = th, tlow, th
    gsum[...] = jnp.zeros_like(gsum)
    msum[...] = jnp.zeros_like(msum)

    mark = lane(9)
    decay = lane(8)
    reach = step_size * axial_speed

    def store_split(a, r):
        h, l = split(state[a * NR + r:a * NR + r + CHUNK, :])
        high[a, r:r + CHUNK, :] = h
        high[a, NR + r:NR + r + CHUNK, :] = h
        high[a, 2 * NR + r:2 * NR + r + CHUNK, :] = l

    def couple(operator):
        for a in range(AX):
            rad[a] = mm(operator[...], high[a])

    def halves(a, r, part):
        lanes_of = slice(0, HALF) if part == 0 else slice(HALF, COEF)
        return high[a, r:r + CHUNK, lanes_of], high[a, 2 * NR + r:2 * NR + r + CHUNK, lanes_of]

    def fold(pc, ps):
        return pc + mark * ps, ps + mark * pc

    def expand_u(a, r):
        ch, cl = halves(a, r, 0)
        sh, sl = halves(a, r, 1)
        eu = mm3(ch, cl, tch[:, 0:HALF], tcl[:, 0:HALF])
        ou = mm3(sh, sl, tsh[:, 0:HALF], tsl[:, 0:HALF])
        return eu, ou

    def slot_v(k):
        return (k + STEPS - 2) % (STEPS - 1)

    def forward_step(k):
        expanded = [None, None]
        fields = [None, None]
        for a in range(AX - 1, -1, -1):
            ch, cl = halves(a, 0, 0)
            sh, sl = halves(a, 0, 1)
            expanded[a] = (mm3(ch, cl, tch[...], tcl[...]), mm3(sh, sl, tsh[...], tsl[...]))
        sw = jnp.concatenate([swirl[...], swirl[...]], 1)
        for a in range(AX - 1, -1, -1):
            rows = slice(a * NR, (a + 1) * NR)
            from_cos, from_sin = expanded[a]
            eu, ov = from_cos[:, 0:HALF], from_cos[:, HALF:]
            ou, ev = from_sin[:, 0:HALF], from_sin[:, HALF:]
            hist_u[k, rows, 0:HALF] = eu
            hist_u[k, rows, HALF:] = ou
            hist_v[slot_v(k), rows, 0:HALF] = ev
            hist_v[slot_v(k), rows, HALF:] = ov
            speed_e = sw + advection_gain * eu
            speed_o = advection_gain * ou
            fields[a] = split(-(speed_e * ev + speed_o * ov)) + split(-(speed_e * ov + speed_o * ev))
            rad[a] = mm(rl[...], high[a])
        for a in range(AX - 1, -1, -1):
            rows = slice(a * NR, (a + 1) * NR)
            geh, gel, goh, gol = fields[a]
            pc, ps = fold(mm3(geh, gel, bch[0:HALF, :], bcl[0:HALF, :]), mm3(goh, gol, bsh[0:HALF, :], bsl[0:HALF, :]))
            force_c, force_s = forced[:, 0:HALF], forced[:, HALF:COEF]
            body_c = turns[k, 0:1, :] * force_c + turns[k, 1:2, :] * force_s
            body_s = turns[k, 2:3, :] * force_c + turns[k, 3:4, :] * force_s
            new_c = decay * state[rows, 0:HALF] + pc + PROFILE[a] * body_c + rad[a, :, 0:HALF]
            new_s = decay * state[rows, HALF:] + ps + PROFILE[a] * body_s + rad[a, :, HALF:]
            if a > 0:
                before = slice(rows.start - NR, rows.stop - NR)
                new_c = new_c + reach * state[before, 0:HALF]
                new_s = new_s + reach * state[before, HALF:]
            state[rows, 0:HALF] = new_c
            state[rows, HALF:] = new_s
            store_split(a, 0)

    tall = lax.broadcasted_iota(jnp.int32, (HALF, OBS), 0).astype(jnp.float32).astype(jnp.bfloat16)
    short = lax.broadcasted_iota(jnp.int32, (AX * QR, OBS), 0)
    one_wide = jnp.ones((HALF, OBS), jnp.bfloat16)
    zero_wide = jnp.zeros((HALF, OBS), jnp.bfloat16)

    def sample(k):
        held = k % STEPS

        dims = (((1,), (1,)), ((), ()))

        def group(first_block):
            blocks = range(first_block, first_block + GROUP)
            ats, values, whiches, picks = [], [], [], []
            for b in blocks:
                block = 2 * b + core
                cell = obs_i[pl.ds(b * STEPS + k - 1, 1), :]
                values.append(obs_v[pl.ds(b * STEPS + k - 1, 1), :])
                column = cell & (NT - 1)
                in_first = column < HALF
                first = jnp.where(in_first, column, -1).astype(jnp.float32).astype(jnp.bfloat16)
                second = jnp.where(in_first, -1, NT - 1 - column).astype(jnp.float32).astype(jnp.bfloat16)
                which = jnp.concatenate(
                    [jnp.where(tall == first, one_wide, zero_wide), jnp.where(tall == second, one_wide, zero_wide)], 0
                )
                whiches.append(which)
                ats.append(short == (cell >> 9))
                parts = []
                for a in range(AX):
                    spot = pl.multiple_of(a * NR + block * QR, 8)
                    eu = hist_u[held, pl.ds(spot, QR), 0:HALF]
                    ou = hist_u[held, pl.ds(spot, QR), HALF:]
                    parts.append(jnp.concatenate([eu + ou, eu - ou], 1))
                uh, ul = split(jnp.concatenate(parts, 0))
                picks.append(mm(jnp.concatenate([uh, ul], 0), which))
            errors, total = [], 0.0
            for at_row, value, picked in zip(ats, values, picks):
                picked = picked[0:AX * QR] + picked[AX * QR:]
                miss = jnp.sum(jnp.where(at_row, picked, 0.0), 0, keepdims=True) - value
                total = total + miss * miss
                eh, el = split(jnp.where(at_row, miss, 0.0))
                errors.append(jnp.concatenate([eh, el], 0))
            backs = [
                lax.dot_general(error, which, dims, preferred_element_type=jnp.float32)
                for error, which in zip(errors, whiches)
            ]
            for b, back in zip(blocks, backs):
                back = (0.5 / step_size) * (back[0:AX * QR] + back[AX * QR:])
                plus, minus = back[:, 0:HALF], back[:, HALF:]
                for a in range(AX):
                    spot = pl.multiple_of(a * NR + (2 * b + core) * QR, 8)
                    idle = pl.multiple_of(a * NR + (2 * b + 1 - core) * QR, 8)
                    own = slice(a * QR, (a + 1) * QR)
                    inject[k - 1, pl.ds(spot, QR), 0:HALF] = plus[own] + minus[own]
                    inject[k - 1, pl.ds(spot, QR), HALF:] = plus[own] - minus[own]
                    inject[k - 1, pl.ds(idle, QR), :] = jnp.zeros((QR, COEF), jnp.float32)
            return total

        for first_block in range(0, BLOCKS // 2, GROUP):
            msum[...] += group(first_block)

    for a in range(AX):
        for r in range(0, NR, CHUNK):
            store_split(a, r)
    forward_step(0)

    def onward(k, carry):
        forward_step(k)
        sample(k)
        return carry

    lax.fori_loop(1, STEPS, onward, 0)
    for a in range(AX):
        for r in range(0, NR, CHUNK):
            rows = slice(a * NR + r, a * NR + r + CHUNK)
            hist_u[0, rows, 0:HALF], hist_u[0, rows, HALF:] = expand_u(a, r)
    sample(STEPS)
    missed = jnp.broadcast_to(jnp.sum(msum[...], 1, keepdims=True), (8, NT))
    keep_out[QR:, :] = missed
    send_out[QR:, :] = missed

    mine = pl.multiple_of(me * QR, 8)
    for a in range(AX):
        spot = pl.multiple_of(a * NR + mine, 8)
        cos_part = state[pl.ds(spot, QR), 0:HALF]
        sin_part = state[pl.ds(spot, QR), HALF:]
        plain_c = cos_part * lane(4) + sin_part * lane(5)
        plain_s = pltpu.roll(cos_part * lane(6) + sin_part * lane(7), 63, 1)
        at_lane = lax.broadcasted_iota(jnp.int32, (QR, 128), 1)
        final_out[a, :, 0:128] = plain_c[:, 0:128]
        final_out[a, :, 128:256] = jnp.where(at_lane < 64, plain_c[:, 128:], plain_s[:, 0:128])
        final_out[a, :, 256:384] = plain_s[:, 128:]

    chip = pl.multiple_of((me - core) * QR, 16)

    def gather_gradient(k):
        wc = jnp.zeros((2 * QR, HALF), jnp.float32)
        ws = wc
        for a in range(AX):
            spot = pl.multiple_of(a * NR + chip, 16)
            wc = wc + (step_size * PROFILE[a]) * state[pl.ds(spot, 2 * QR), 0:HALF]
            ws = ws + (step_size * PROFILE[a]) * state[pl.ds(spot, 2 * QR), HALF:]
        gsum[:, 0:HALF] += turns[k, 4:5, :] * wc + turns[k, 5:6, :] * ws
        gsum[:, HALF:] += turns[k, 6:7, :] * wc + turns[k, 7:8, :] * ws

    for a in range(AX):
        for r in range(0, NR, CHUNK):
            rows = slice(a * NR + r, a * NR + r + CHUNK)
            eh, el = split(inject[STEPS - 1, rows, 0:HALF])
            oh, ol = split(inject[STEPS - 1, rows, HALF:])
            lc, ls = fold(mm3(eh, el, bch[0:HALF, :], bcl[0:HALF, :]), mm3(oh, ol, bsh[0:HALF, :], bsl[0:HALF, :]))
            state[rows, 0:HALF] = lc
            state[rows, HALF:] = ls
            store_split(a, r)

    def pull_back(k, a, rows, sw, eq, oq, coupled):
        gather_back(a, rows, weigh(k, rows, sw, eq, oq), coupled)

    def weigh(k, rows, sw, eq, oq):
        eu, ou = hist_u[k, rows, 0:HALF], hist_u[k, rows, HALF:]
        ev, ov = hist_v[slot_v(k), rows, 0:HALF], hist_v[slot_v(k), rows, HALF:]
        speed_e = sw + advection_gain * eu
        speed_o = advection_gain * ou
        tve = -(speed_e * eq + speed_o * oq)
        tvo = -(speed_e * oq + speed_o * eq)
        eq = advection_gain * eq
        oq = advection_gain * oq
        tue = inject[k - 1, rows, 0:HALF] - (ev * eq + ov * oq)
        tuo = inject[k - 1, rows, HALF:] - (ev * oq + ov * eq)
        return split(tue) + split(tuo) + split(tve) + split(tvo)

    def gather_back(a, rows, fields, coupled):
        ueh, uel, uoh, uol, veh, vel, voh, vol = fields
        pc = mm3(ueh, uel, bch[0:HALF, :], bcl[0:HALF, :]) + mm3(voh, vol, bch[HALF:, :], bcl[HALF:, :])
        ps = mm3(uoh, uol, bsh[0:HALF, :], bsl[0:HALF, :]) + mm3(veh, vel, bsh[HALF:, :], bsl[HALF:, :])
        pc, ps = fold(pc, ps)
        new_c = decay * state[rows, 0:HALF] + pc + coupled[:, 0:HALF]
        new_s = decay * state[rows, HALF:] + ps + coupled[:, HALF:]
        if a < AX - 1:
            if isinstance(rows, slice):
                after = slice(rows.start + NR, rows.stop + NR)
            else:
                after = pl.ds(pl.multiple_of((a + 1) * NR + chip, 8), 2 * QR)
            new_c = new_c + reach * state[after, 0:HALF]
            new_s = new_s + reach * state[after, HALF:]
        state[rows, 0:HALF] = new_c
        state[rows, HALF:] = new_s

    def backward_step(k):
        synthesized = [expand_u(a, 0) for a in range(AX)]
        sw = jnp.concatenate([swirl[...], swirl[...]], 1)
        fields = []
        for a in range(AX):
            rows = slice(a * NR, (a + 1) * NR)
            fields.append(weigh(k, rows, sw, *synthesized[a]))
            rad[a] = mm(rtl[...], high[a])
        for a in range(AX):
            rows = slice(a * NR, (a + 1) * NR)
            gather_back(a, rows, fields[a], rad[a])
            store_split(a, 0)

    def backward_chip():
        part = pl.ds(chip, 2 * QR)
        sw = jnp.concatenate([swirl[part, :], swirl[part, :]], 1)
        for a in range(AX):
            rows = pl.ds(pl.multiple_of(a * NR + chip, 16), 2 * QR)
            coupled = mm(rtl[part, :], high[a])
            ahead = high[a, part, :]
            rest = high[a, pl.ds(pl.multiple_of(2 * NR + chip, 16), 2 * QR), :]
            eq = mm3(ahead[:, 0:HALF], rest[:, 0:HALF], tch[:, 0:HALF], tcl[:, 0:HALF])
            oq = mm3(ahead[:, HALF:], rest[:, HALF:], tsh[:, 0:HALF], tsl[:, 0:HALF])
            pull_back(1, a, rows, sw, eq, oq, coupled)

    def inward(i, carry):
        k = STEPS - 1 - i
        gather_gradient(k)
        backward_step(k)
        return carry

    lax.fori_loop(0, STEPS - 2, inward, 0)
    gather_gradient(1)
    backward_chip()
    gather_gradient(0)
    gh, gl = split(gsum[...])
    gsum[...] = mm3(gh, gl, gth[...], gtl[...])
    keep_out[0:QR, :] = gsum[pl.ds(pl.multiple_of(core * QR, 8), QR), :]
    send_out[0:QR, :] = gsum[pl.ds(pl.multiple_of((1 - core) * QR, 8), QR), :]


def window_step(place, turns, radial_op, pieces):
    from_cos, from_sin = half_tables()
    whole = whole_table()
    tables = []
    for table in (from_cos, from_sin, 2.0 * step_size * from_cos.T, 2.0 * step_size * from_sin.T, whole.T, whole):
        tables += [jnp.asarray(part) for part in split_np(table)]
    operands = [place, turns, jnp.asarray(lane_rows()), radial_op, *tables, *pieces]
    vmem = pl.BlockSpec(memory_space=pltpu.VMEM)
    f32, bf16 = jnp.float32, jnp.bfloat16
    return pl.pallas_call(
        kernel,
        out_shape=(
            jax.ShapeDtypeStruct((AX, QR, 384), f32),
            jax.ShapeDtypeStruct((QR + 8, NT), f32),
            jax.ShapeDtypeStruct((QR + 8, NT), f32),
        ),
        in_specs=[pl.BlockSpec(memory_space=pltpu.SMEM)] + [vmem] * (len(operands) - 1),
        out_specs=(vmem, vmem, vmem),
        scratch_shapes=[
            pltpu.VMEM((ROWS, COEF), f32),
            pltpu.VMEM((AX, 3 * NR, COEF), bf16),
            pltpu.VMEM((AX, NR, COEF), f32),
            pltpu.VMEM((STEPS, ROWS, COEF), f32),
            pltpu.VMEM((STEPS - 1, ROWS, COEF), f32),
            pltpu.VMEM((STEPS, ROWS, COEF), f32),
            pltpu.VMEM((NR, 3 * NR), bf16),
            pltpu.VMEM((NR, 3 * NR), bf16),
            pltpu.VMEM((NR, 128), f32),
            pltpu.VMEM((NR, COEF), f32),
            pltpu.VMEM((BLOCKS // 2 * STEPS, OBS), jnp.int32),
            pltpu.VMEM((BLOCKS // 2 * STEPS, OBS), f32),
            pltpu.VMEM((2 * QR, COEF), f32),
            pltpu.VMEM((1, OBS), f32),
        ],
        compiler_params=pltpu.CompilerParams(vmem_limit_bytes=VMEM_LIMIT),
    )(*operands)


def pack_kernel(guess, forcing, swirl, cells, values, out):
    for a in range(AX):
        out[:, 384 * a:384 * (a + 1)] = guess[0, a]
    out[:, 768:1280] = forcing[...]
    out[0:8, 1280:1536] = cells[0].astype(jnp.float32)
    out[8:16, 1280:1536] = values[0]
    out[16:24, 1280:1408] = jnp.broadcast_to(swirl[...], (8, 128))
    out[16:24, 1408:1536] = jnp.zeros((8, 128), jnp.float32)


def pack(first_guess, forcing, swirl, obs_index, obs_value):
    padded = jnp.pad(swirl[None, :], ((0, 0), (0, 128 - QR)))
    vmem = pl.BlockSpec(memory_space=pltpu.VMEM)
    return pl.pallas_call(
        pack_kernel,
        out_shape=jax.ShapeDtypeStruct((QR, 1536), jnp.float32),
        in_specs=[vmem] * 5,
        out_specs=vmem,
    )(first_guess, forcing, padded, obs_index, obs_value)


def per_device(first_guess, forcing, swirl, radial_op, obs_index, obs_value, start_step):
    me = lax.axis_index("space")

    def space_swap(x, bits):
        return lax.ppermute(x, "space", [(i, i ^ bits) for i in range(BLOCKS)])

    def space_turn(x, d):
        return lax.ppermute(x, "space", [(i, i // 8 * 8 + (i + 2 * d) % 8) for i in range(BLOCKS)])

    def win_send(x, where):
        return lax.ppermute(x, "win", [(i, where(i)) for i in range(16)])

    message = pack(first_guess, forcing, swirl, obs_index, obs_value)
    other_x = space_swap(message, 8)
    both = jnp.concatenate([message, other_x], 0)
    left, right = space_turn(both, 1), space_turn(both, 3)
    early = [space_swap(message, 1), space_swap(other_x, 1)]
    turns = turn_tables(start_step[0])
    left, right, ahead, behind, turns = lax.optimization_barrier((left, right, left[:QR], right[QR:], turns))
    opposite = [space_turn(ahead, 1), space_turn(behind, 3)]
    left, right, opposite = lax.optimization_barrier((left, right, opposite))
    pieces = [message, other_x, left, right, *opposite]
    pieces += early + [space_swap(piece, 1) for piece in pieces[2:]]

    final, keep, send = window_step(me.astype(jnp.int32).reshape(1), turns, radial_op, pieces)

    both_cores = keep + space_swap(send, 1)
    misfit = both_cores[QR, 0:1] * (0.5 / (STEPS * BLOCKS * OBS))
    total = both_cores[0:QR]
    near = [win_send(total, lambda i, f=f: i ^ f) for f in (1, 2, 3)]
    total = total + near[0] + near[1] + near[2]
    far = [win_send(total, lambda i, d=d: (i + 2 * d) % 16) for d in (2, 4, 6)]
    total = total + far[0] + far[1] + far[2]
    return final[None], misfit, total


def solution(mesh):
    return jax.shard_map(
        per_device,
        mesh=mesh,
        in_specs=(
            P("win", None, "space", None),
            P("space", None),
            P("space"),
            P(),
            P("win", None, "space"),
            P("win", None, "space"),
            P("win"),
        ),
        out_specs=(P("win", None, "space", None), P("win"), P("space", None)),
        check_vma=False,
    )
```

```python
import math

import jax
import jax.numpy as jnp
import ml_dtypes
import numpy as np
from jax import lax
from jax.experimental import pallas as pl
from jax.experimental.pallas import tpu as pltpu
from jax.sharding import PartitionSpec as P

MODES = 192
STEPS = 8
ROT = 8
NT = 512
NR = 384
AX = 2
HALF = NT // 2
BLOCKS = 16
QR = NR // BLOCKS
OBS = 256
ROWS = AX * NR
COEF = 2 * HALF
GROUP = 8
CHUNK = 384
VMEM_LIMIT = 60 * 1024 * 1024

step_size = 0.25
radial_scale = 0.4
radial_damping = 0.4
axial_speed = 0.4
advection_gain = 0.2
PROFILE = [math.exp(-(((a + 0.5 - AX / 2.0) * (4.0 / AX)) ** 2)) for a in range(AX)]

OMEGA = 2.0 * math.pi / NT
PHI = OMEGA * np.arange(HALF) / 2.0


def split_np(table):
    high = table.astype(ml_dtypes.bfloat16)
    low = (table - high.astype(np.float64)).astype(ml_dtypes.bfloat16)
    return high, low


def half_tables():
    m = np.arange(HALF)[:, None].astype(np.float64)
    theta = np.arange(HALF)[None, :] + 0.5
    norm = np.where(m == 0, 1.0 / math.sqrt(NT), math.sqrt(2.0 / NT))
    cosine = norm * np.cos(OMEGA * m * theta)
    sine = norm * np.sin(OMEGA * m * theta)
    slope = OMEGA * m
    kept = m < MODES
    last = m == MODES
    sin_phi, cos_phi = math.sin(PHI[MODES]), math.cos(PHI[MODES])
    even_u = np.where(kept, cosine, np.where(last, -sin_phi * cosine, 0.0))
    odd_u = np.where(kept & (m > 0), sine, np.where(last, cos_phi * sine, 0.0))
    odd_v = np.where(kept, -slope * sine, np.where(last, sin_phi * slope * sine, 0.0))
    even_v = np.where(kept & (m > 0), slope * cosine, np.where(last, cos_phi * slope * cosine, 0.0))
    from_cos = np.concatenate([even_u, odd_v], 1)
    from_sin = np.concatenate([odd_u, even_v], 1)
    return from_cos, from_sin


def whole_table():
    m = np.arange(HALF)[:, None].astype(np.float64)
    theta = np.arange(NT)[None, :] + 0.5
    norm = np.where(m == 0, 1.0 / math.sqrt(NT), math.sqrt(2.0 / NT))
    cosine = np.where(m <= MODES, norm * np.cos(OMEGA * m * theta), 0.0)
    sine = np.where((m <= MODES) & (m > 0), norm * np.sin(OMEGA * m * theta), 0.0)
    return np.concatenate([cosine, sine], 0)


def lane_rows():
    m = np.arange(HALF)
    kept = (m >= 1) & (m < MODES)
    last = m == MODES
    cos_phi, sin_phi = np.cos(PHI), np.sin(PHI)
    rows = np.zeros((16, HALF))
    rows[0] = np.where(kept, cos_phi, np.where(m == 0, 1.0, 0.0))
    rows[1] = np.where(kept, -sin_phi, np.where(last, 1.0, 0.0))
    rows[2] = np.where(kept, sin_phi, 0.0)
    rows[3] = np.where(kept, cos_phi, np.where(last, 1.0, 0.0))
    rows[4] = np.where(kept, cos_phi, np.where(m == 0, 1.0, 0.0))
    rows[5] = np.where(kept, sin_phi, 0.0)
    rows[6] = np.where(kept, -sin_phi, 0.0)
    rows[7] = np.where(kept, cos_phi, np.where(last, 1.0, 0.0))
    rows[8] = np.where(m <= MODES, 1.0 - step_size * (radial_damping + axial_speed + (m / MODES) ** 2), 0.0)
    rows[9] = np.where(last, 1.0, 0.0)
    return rows.astype(np.float32)


def turn_tables(phase_start):
    m = jnp.arange(HALF, dtype=jnp.int32)[None, :]
    cells = ROT * (phase_start + jnp.arange(STEPS, dtype=jnp.int32))[:, None]
    angles = OMEGA * ((m * cells) % NT).astype(jnp.float32)
    cosine, sine = jnp.cos(angles), jnp.sin(angles)
    sin_phi, cos_phi = math.sin(PHI[MODES]), math.cos(PHI[MODES])
    last = m == MODES
    first = -sin_phi * cosine + cos_phi * sine
    second = sin_phi * sine + cos_phi * cosine
    forward = [
        jnp.where(last, first, cosine),
        jnp.where(last, second, -sine),
        jnp.where(last, first, sine),
        jnp.where(last, second, cosine),
    ]
    back = [
        forward[0],
        jnp.where(last, 0.0, sine),
        forward[1],
        jnp.where(last, 0.0, cosine),
    ]
    keep = (m <= MODES).astype(jnp.float32)
    return jnp.stack([row * keep for row in forward + back], 1)


def split(x):
    high = x.astype(jnp.bfloat16)
    return high, (x - high.astype(jnp.float32)).astype(jnp.bfloat16)


def mm(a, b):
    return jnp.dot(a, b, preferred_element_type=jnp.float32)


def mm3(xh, xl, th, tl):
    return mm(xh, th) + mm(xl, th) + mm(xh, tl)


def kernel(
    place, turns, lanes, radial_op, tch, tcl, tsh, tsl, bch, bcl, bsh, bsl, fth, ftl, gth, gtl,
    p0, p1, p2, p3, p4, p5, q0, q1, q2, q3, q4, q5,
    final_out, keep_out, send_out,
    state, high, rad, hist_u, hist_v, inject, rl, rtl, swirl, forced, obs_i, obs_v, gsum, msum,
):
    me = place[0]
    core = me % 2
    across = me // 8
    up = (me // 2) % 4

    def block_of(d, flip_x, flip_core):
        y = (up + 4 - d) % 4
        x = 1 - across if flip_x else across
        c = 1 - core if flip_core else core
        return x * 8 + y * 2 + c

    sources = [(p0, 0, 0, False, False), (p1, 0, 0, True, False), (q0, 0, 0, False, True), (q1, 0, 0, True, True)]
    for d, pd, qd in ((1, p2, q2), (3, p3, q3)):
        sources += [(pd, 0, d, False, False), (pd, QR, d, True, False), (qd, 0, d, False, True), (qd, QR, d, True, True)]
    sources += [(p4, 0, 2, False, False), (p5, 0, 2, True, False), (q4, 0, 2, False, True), (q5, 0, 2, True, True)]

    def lane(i):
        return lanes[i:i + 1, :]

    square = lax.broadcasted_iota(jnp.int32, (QR, 128), 0) == lax.broadcasted_iota(jnp.int32, (QR, 128), 1)
    for ref, row, d, flip_x, flip_core in sources:
        block = block_of(d, flip_x, flip_core)
        at = pl.multiple_of(block * QR, 8)
        for a in range(AX):
            first = ref[row:row + QR, 384 * a:384 * a + HALF]
            second = pltpu.roll(ref[row:row + QR, 384 * a + 128:384 * a + 384], 193, 1)
            spot = pl.multiple_of(a * NR + at, 8)
            state[pl.ds(spot, QR), 0:HALF] = first * lane(0) + second * lane(1)
            state[pl.ds(spot, QR), HALF:COEF] = first * lane(2) + second * lane(3)
        forced[pl.ds(at, QR), :] = ref[row:row + QR, 768:1280]
        spread = jnp.where(square, ref[row + 16:row + 17, 1280:1408], 0.0)
        swirl[pl.ds(at, QR), :] = jnp.broadcast_to(jnp.sum(spread, 1, keepdims=True), (QR, 128))
        if not flip_core:
            slot = pl.multiple_of((block // 2) * STEPS, 8)
            obs_i[pl.ds(slot, STEPS), :] = ref[row:row + 8, 1280:1536].astype(jnp.int32)
            obs_v[pl.ds(slot, STEPS), :] = ref[row + 8:row + 16, 1280:1536]

    fh, fl = split(forced[...])
    forced[...] = mm3(fh, fl, fth[...], ftl[...]) * step_size

    scaled = (step_size * radial_scale) * radial_op[...]
    rh, rlow = split(scaled)
    rl[:, 0:NR], rl[:, NR:2 * NR], rl[:, 2 * NR:] = rh, rlow, rh
    th, tlow = split(scaled.T)
    rtl[:, 0:NR], rtl[:, NR:2 * NR], rtl[:, 2 * NR:] = th, tlow, th
    gsum[...] = jnp.zeros_like(gsum)
    msum[...] = jnp.zeros_like(msum)

    mark = lane(9)
    decay = lane(8)
    reach = step_size * axial_speed

    def store_split(a, r):
        h, l = split(state[a * NR + r:a * NR + r + CHUNK, :])
        high[a, r:r + CHUNK, :] = h
        high[a, NR + r:NR + r + CHUNK, :] = h
        high[a, 2 * NR + r:2 * NR + r + CHUNK, :] = l

    def couple(operator):
        for a in range(AX):
            rad[a] = mm(operator[...], high[a])

    def halves(a, r, part):
        lanes_of = slice(0, HALF) if part == 0 else slice(HALF, COEF)
        return high[a, r:r + CHUNK, lanes_of], high[a, 2 * NR + r:2 * NR + r + CHUNK, lanes_of]

    def fold(pc, ps):
        return pc + mark * ps, ps + mark * pc

    def expand_u(a, r):
        ch, cl = halves(a, r, 0)
        sh, sl = halves(a, r, 1)
        eu = mm3(ch, cl, tch[:, 0:HALF], tcl[:, 0:HALF])
        ou = mm3(sh, sl, tsh[:, 0:HALF], tsl[:, 0:HALF])
        return eu, ou

    def slot_v(k):
        return (k + STEPS - 2) % (STEPS - 1)

    def forward_step(k):
        expanded = [None, None]
        fields = [None, None]
        for a in range(AX - 1, -1, -1):
            ch, cl = halves(a, 0, 0)
            sh, sl = halves(a, 0, 1)
            expanded[a] = (mm3(ch, cl, tch[...], tcl[...]), mm3(sh, sl, tsh[...], tsl[...]))
        sw = jnp.concatenate([swirl[...], swirl[...]], 1)
        for a in range(AX - 1, -1, -1):
            rows = slice(a * NR, (a + 1) * NR)
            from_cos, from_sin = expanded[a]
            eu, ov = from_cos[:, 0:HALF], from_cos[:, HALF:]
            ou, ev = from_sin[:, 0:HALF], from_sin[:, HALF:]
            hist_u[k, rows, 0:HALF] = eu
            hist_u[k, rows, HALF:] = ou
            hist_v[slot_v(k), rows, 0:HALF] = ev
            hist_v[slot_v(k), rows, HALF:] = ov
            speed_e = sw + advection_gain * eu
            speed_o = advection_gain * ou
            fields[a] = split(-(speed_e * ev + speed_o * ov)) + split(-(speed_e * ov + speed_o * ev))
            rad[a] = mm(rl[...], high[a])
        for a in range(AX - 1, -1, -1):
            rows = slice(a * NR, (a + 1) * NR)
            geh, gel, goh, gol = fields[a]
            pc, ps = fold(mm3(geh, gel, bch[0:HALF, :], bcl[0:HALF, :]), mm3(goh, gol, bsh[0:HALF, :], bsl[0:HALF, :]))
            force_c, force_s = forced[:, 0:HALF], forced[:, HALF:COEF]
            body_c = turns[k, 0:1, :] * force_c + turns[k, 1:2, :] * force_s
            body_s = turns[k, 2:3, :] * force_c + turns[k, 3:4, :] * force_s
            new_c = decay * state[rows, 0:HALF] + pc + PROFILE[a] * body_c + rad[a, :, 0:HALF]
            new_s = decay * state[rows, HALF:] + ps + PROFILE[a] * body_s + rad[a, :, HALF:]
            if a > 0:
                before = slice(rows.start - NR, rows.stop - NR)
                new_c = new_c + reach * state[before, 0:HALF]
                new_s = new_s + reach * state[before, HALF:]
            state[rows, 0:HALF] = new_c
            state[rows, HALF:] = new_s
            store_split(a, 0)

    tall = lax.broadcasted_iota(jnp.int32, (HALF, OBS), 0).astype(jnp.float32).astype(jnp.bfloat16)
    short = lax.broadcasted_iota(jnp.int32, (AX * QR, OBS), 0)
    one_wide = jnp.ones((HALF, OBS), jnp.bfloat16)
    zero_wide = jnp.zeros((HALF, OBS), jnp.bfloat16)

    def sample(k):
        held = k % STEPS

        dims = (((1,), (1,)), ((), ()))

        def group(first_block):
            blocks = range(first_block, first_block + GROUP)
            ats, values, whiches, picks = [], [], [], []
            for b in blocks:
                block = 2 * b + core
                cell = obs_i[pl.ds(b * STEPS + k - 1, 1), :]
                values.append(obs_v[pl.ds(b * STEPS + k - 1, 1), :])
                column = cell & (NT - 1)
                in_first = column < HALF
                first = jnp.where(in_first, column, -1).astype(jnp.float32).astype(jnp.bfloat16)
                second = jnp.where(in_first, -1, NT - 1 - column).astype(jnp.float32).astype(jnp.bfloat16)
                which = jnp.concatenate(
                    [jnp.where(tall == first, one_wide, zero_wide), jnp.where(tall == second, one_wide, zero_wide)], 0
                )
                whiches.append(which)
                ats.append(short == (cell >> 9))
                parts = []
                for a in range(AX):
                    spot = pl.multiple_of(a * NR + block * QR, 8)
                    eu = hist_u[held, pl.ds(spot, QR), 0:HALF]
                    ou = hist_u[held, pl.ds(spot, QR), HALF:]
                    parts.append(jnp.concatenate([eu + ou, eu - ou], 1))
                uh, ul = split(jnp.concatenate(parts, 0))
                picks.append(mm(jnp.concatenate([uh, ul], 0), which))
            errors, total = [], 0.0
            for at_row, value, picked in zip(ats, values, picks):
                picked = picked[0:AX * QR] + picked[AX * QR:]
                miss = jnp.sum(jnp.where(at_row, picked, 0.0), 0, keepdims=True) - value
                total = total + miss * miss
                eh, el = split(jnp.where(at_row, miss, 0.0))
                errors.append(jnp.concatenate([eh, el], 0))
            backs = [
                lax.dot_general(error, which, dims, preferred_element_type=jnp.float32)
                for error, which in zip(errors, whiches)
            ]
            for b, back in zip(blocks, backs):
                back = (0.5 / step_size) * (back[0:AX * QR] + back[AX * QR:])
                plus, minus = back[:, 0:HALF], back[:, HALF:]
                for a in range(AX):
                    spot = pl.multiple_of(a * NR + (2 * b + core) * QR, 8)
                    idle = pl.multiple_of(a * NR + (2 * b + 1 - core) * QR, 8)
                    own = slice(a * QR, (a + 1) * QR)
                    inject[k - 1, pl.ds(spot, QR), 0:HALF] = plus[own] + minus[own]
                    inject[k - 1, pl.ds(spot, QR), HALF:] = plus[own] - minus[own]
                    inject[k - 1, pl.ds(idle, QR), :] = jnp.zeros((QR, COEF), jnp.float32)
            return total

        for first_block in range(0, BLOCKS // 2, GROUP):
            msum[...] += group(first_block)

    for a in range(AX):
        for r in range(0, NR, CHUNK):
            store_split(a, r)
    forward_step(0)

    def onward(k, carry):
        forward_step(k)
        sample(k)
        return carry

    lax.fori_loop(1, STEPS, onward, 0)
    for a in range(AX):
        for r in range(0, NR, CHUNK):
            rows = slice(a * NR + r, a * NR + r + CHUNK)
            hist_u[0, rows, 0:HALF], hist_u[0, rows, HALF:] = expand_u(a, r)
    sample(STEPS)
    missed = jnp.broadcast_to(jnp.sum(msum[...], 1, keepdims=True), (8, NT))
    keep_out[QR:, :] = missed
    send_out[QR:, :] = missed

    mine = pl.multiple_of(me * QR, 8)
    for a in range(AX):
        spot = pl.multiple_of(a * NR + mine, 8)
        cos_part = state[pl.ds(spot, QR), 0:HALF]
        sin_part = state[pl.ds(spot, QR), HALF:]
        plain_c = cos_part * lane(4) + sin_part * lane(5)
        plain_s = pltpu.roll(cos_part * lane(6) + sin_part * lane(7), 63, 1)
        at_lane = lax.broadcasted_iota(jnp.int32, (QR, 128), 1)
        final_out[a, :, 0:128] = plain_c[:, 0:128]
        final_out[a, :, 128:256] = jnp.where(at_lane < 64, plain_c[:, 128:], plain_s[:, 0:128])
        final_out[a, :, 256:384] = plain_s[:, 128:]

    chip = pl.multiple_of((me - core) * QR, 16)

    def gather_gradient(k):
        wc = jnp.zeros((2 * QR, HALF), jnp.float32)
        ws = wc
        for a in range(AX):
            spot = pl.multiple_of(a * NR + chip, 16)
            wc = wc + (step_size * PROFILE[a]) * state[pl.ds(spot, 2 * QR), 0:HALF]
            ws = ws + (step_size * PROFILE[a]) * state[pl.ds(spot, 2 * QR), HALF:]
        gsum[:, 0:HALF] += turns[k, 4:5, :] * wc + turns[k, 5:6, :] * ws
        gsum[:, HALF:] += turns[k, 6:7, :] * wc + turns[k, 7:8, :] * ws

    for a in range(AX):
        for r in range(0, NR, CHUNK):
            rows = slice(a * NR + r, a * NR + r + CHUNK)
            eh, el = split(inject[STEPS - 1, rows, 0:HALF])
            oh, ol = split(inject[STEPS - 1, rows, HALF:])
            lc, ls = fold(mm3(eh, el, bch[0:HALF, :], bcl[0:HALF, :]), mm3(oh, ol, bsh[0:HALF, :], bsl[0:HALF, :]))
            state[rows, 0:HALF] = lc
            state[rows, HALF:] = ls
            store_split(a, r)

    def pull_back(k, a, rows, sw, eq, oq, coupled):
        gather_back(a, rows, weigh(k, rows, sw, eq, oq), coupled)

    def weigh(k, rows, sw, eq, oq):
        eu, ou = hist_u[k, rows, 0:HALF], hist_u[k, rows, HALF:]
        ev, ov = hist_v[slot_v(k), rows, 0:HALF], hist_v[slot_v(k), rows, HALF:]
        speed_e = sw + advection_gain * eu
        speed_o = advection_gain * ou
        tve = -(speed_e * eq + speed_o * oq)
        tvo = -(speed_e * oq + speed_o * eq)
        eq = advection_gain * eq
        oq = advection_gain * oq
        tue = inject[k - 1, rows, 0:HALF] - (ev * eq + ov * oq)
        tuo = inject[k - 1, rows, HALF:] - (ev * oq + ov * eq)
        return split(tue) + split(tuo) + split(tve) + split(tvo)

    def gather_back(a, rows, fields, coupled):
        ueh, uel, uoh, uol, veh, vel, voh, vol = fields
        pc = mm3(ueh, uel, bch[0:HALF, :], bcl[0:HALF, :]) + mm3(voh, vol, bch[HALF:, :], bcl[HALF:, :])
        ps = mm3(uoh, uol, bsh[0:HALF, :], bsl[0:HALF, :]) + mm3(veh, vel, bsh[HALF:, :], bsl[HALF:, :])
        pc, ps = fold(pc, ps)
        new_c = decay * state[rows, 0:HALF] + pc + coupled[:, 0:HALF]
        new_s = decay * state[rows, HALF:] + ps + coupled[:, HALF:]
        if a < AX - 1:
            if isinstance(rows, slice):
                after = slice(rows.start + NR, rows.stop + NR)
            else:
                after = pl.ds(pl.multiple_of((a + 1) * NR + chip, 8), 2 * QR)
            new_c = new_c + reach * state[after, 0:HALF]
            new_s = new_s + reach * state[after, HALF:]
        state[rows, 0:HALF] = new_c
        state[rows, HALF:] = new_s

    def backward_step(k):
        synthesized = [expand_u(a, 0) for a in range(AX)]
        sw = jnp.concatenate([swirl[...], swirl[...]], 1)
        fields = []
        for a in range(AX):
            rows = slice(a * NR, (a + 1) * NR)
            fields.append(weigh(k, rows, sw, *synthesized[a]))
            rad[a] = mm(rtl[...], high[a])
        for a in range(AX):
            rows = slice(a * NR, (a + 1) * NR)
            gather_back(a, rows, fields[a], rad[a])
            store_split(a, 0)

    def backward_chip():
        part = pl.ds(chip, 2 * QR)
        sw = jnp.concatenate([swirl[part, :], swirl[part, :]], 1)
        for a in range(AX):
            rows = pl.ds(pl.multiple_of(a * NR + chip, 16), 2 * QR)
            coupled = mm(rtl[part, :], high[a])
            ahead = high[a, part, :]
            rest = high[a, pl.ds(pl.multiple_of(2 * NR + chip, 16), 2 * QR), :]
            eq = mm3(ahead[:, 0:HALF], rest[:, 0:HALF], tch[:, 0:HALF], tcl[:, 0:HALF])
            oq = mm3(ahead[:, HALF:], rest[:, HALF:], tsh[:, 0:HALF], tsl[:, 0:HALF])
            pull_back(1, a, rows, sw, eq, oq, coupled)

    def inward(i, carry):
        k = STEPS - 1 - i
        gather_gradient(k)
        backward_step(k)
        return carry

    lax.fori_loop(0, STEPS - 2, inward, 0)
    gather_gradient(1)
    backward_chip()
    gather_gradient(0)
    gh, gl = split(gsum[...])
    gsum[...] = mm3(gh, gl, gth[...], gtl[...])
    keep_out[0:QR, :] = gsum[pl.ds(pl.multiple_of(core * QR, 8), QR), :]
    send_out[0:QR, :] = gsum[pl.ds(pl.multiple_of((1 - core) * QR, 8), QR), :]


def window_step(place, turns, radial_op, pieces):
    from_cos, from_sin = half_tables()
    whole = whole_table()
    tables = []
    for table in (from_cos, from_sin, 2.0 * step_size * from_cos.T, 2.0 * step_size * from_sin.T, whole.T, whole):
        tables += [jnp.asarray(part) for part in split_np(table)]
    operands = [place, turns, jnp.asarray(lane_rows()), radial_op, *tables, *pieces]
    vmem = pl.BlockSpec(memory_space=pltpu.VMEM)
    f32, bf16 = jnp.float32, jnp.bfloat16
    return pl.pallas_call(
        kernel,
        out_shape=(
            jax.ShapeDtypeStruct((AX, QR, 384), f32),
            jax.ShapeDtypeStruct((QR + 8, NT), f32),
            jax.ShapeDtypeStruct((QR + 8, NT), f32),
        ),
        in_specs=[pl.BlockSpec(memory_space=pltpu.SMEM)] + [vmem] * (len(operands) - 1),
        out_specs=(vmem, vmem, vmem),
        scratch_shapes=[
            pltpu.VMEM((ROWS, COEF), f32),
            pltpu.VMEM((AX, 3 * NR, COEF), bf16),
            pltpu.VMEM((AX, NR, COEF), f32),
            pltpu.VMEM((STEPS, ROWS, COEF), f32),
            pltpu.VMEM((STEPS - 1, ROWS, COEF), f32),
            pltpu.VMEM((STEPS, ROWS, COEF), f32),
            pltpu.VMEM((NR, 3 * NR), bf16),
            pltpu.VMEM((NR, 3 * NR), bf16),
            pltpu.VMEM((NR, 128), f32),
            pltpu.VMEM((NR, COEF), f32),
            pltpu.VMEM((BLOCKS // 2 * STEPS, OBS), jnp.int32),
            pltpu.VMEM((BLOCKS // 2 * STEPS, OBS), f32),
            pltpu.VMEM((2 * QR, COEF), f32),
            pltpu.VMEM((1, OBS), f32),
        ],
        compiler_params=pltpu.CompilerParams(vmem_limit_bytes=VMEM_LIMIT),
    )(*operands)


def per_device(first_guess, forcing, swirl, radial_op, obs_index, obs_value, start_step):
    me = lax.axis_index("space")

    def space_swap(x, bits):
        return lax.ppermute(x, "space", [(i, i ^ bits) for i in range(BLOCKS)])

    def space_turn(x, d):
        return lax.ppermute(x, "space", [(i, i // 8 * 8 + (i + 2 * d) % 8) for i in range(BLOCKS)])

    def win_send(x, where):
        return lax.ppermute(x, "win", [(i, where(i)) for i in range(16)])

    extra = jnp.concatenate(
        [
            obs_index[0].astype(jnp.float32),
            obs_value[0],
            jnp.pad(swirl[None, :], ((0, 7), (0, OBS - QR))),
        ],
        0,
    )
    message = jnp.concatenate([first_guess[0, 0], first_guess[0, 1], forcing, extra], 1)
    other_x = space_swap(message, 8)
    both = jnp.concatenate([message, other_x], 0)
    left, right = space_turn(both, 1), space_turn(both, 3)
    turns = turn_tables(start_step[0])
    left, right, ahead, behind, turns = lax.optimization_barrier((left, right, left[:QR], right[QR:], turns))
    opposite = [space_turn(ahead, 1), space_turn(behind, 3)]
    pieces = list(lax.optimization_barrier((message, other_x, left, right, *opposite)))
    pieces += [space_swap(piece, 1) for piece in pieces]

    final, keep, send = window_step(me.astype(jnp.int32).reshape(1), turns, radial_op, pieces)

    both_cores = keep + space_swap(send, 1)
    misfit = both_cores[QR, 0:1] * (0.5 / (STEPS * BLOCKS * OBS))
    total = both_cores[0:QR]
    near = [win_send(total, lambda i, f=f: i ^ f) for f in (1, 2, 3)]
    total = total + near[0] + near[1] + near[2]
    far = [win_send(total, lambda i, d=d: (i + 2 * d) % 16) for d in (2, 4, 6)]
    total = total + far[0] + far[1] + far[2]
    return final[None], misfit, total


def solution(mesh):
    return jax.shard_map(
        per_device,
        mesh=mesh,
        in_specs=(
            P("win", None, "space", None),
            P("space", None),
            P("space"),
            P(),
            P("win", None, "space"),
            P("win", None, "space"),
            P("win"),
        ),
        out_specs=(P("win", None, "space", None), P("win"), P("space", None)),
        check_vma=False,
    )
```
